256 devices in a mesh: mem: 8 (over y, core), ctx: 32 (over z, x).
Axes of the slice: x: 4, y: 4, z: 8, core: 2. Of those that a mesh axis runs over, the one named last changes fastest.
Arguments:
- queries: bfloat16 [32, 1024, 32, 128], P('ctx', 'mem'), may hold values from -6 to 6
- keys: bfloat16 [32, 1024, 32, 128], P('ctx', 'mem'), may hold values from -6 to 6
- values: bfloat16 [32, 1024, 32, 128], P('ctx', 'mem'), may hold values from -6 to 6
- log_decay: bfloat16 [32, 1024, 32], P('ctx', 'mem'), may hold values from -1 to 0, as said below
- routes: int32 [32, 1024, 2], P('ctx', 'mem'), may hold values from 0 to 7, all different within a row; in each aligned block of 128 rows (0 to 127, 128 to 255, ..., all dimensions but the last counted through in order) at most 40 rows name the same one
- route_weight: float32 [32, 1024, 2], P('ctx', 'mem'), may hold values from 0.2 to 1
- gain: float32 [4096], replicated, may hold values from 0.25 to 1.75
Outputs:
- layer_out: bfloat16 [32, 1024, 32, 128], P('ctx', 'mem')
The draws below stay inside these ranges and needn't reach their ends.
Inputs may be any that keep to these rules, and one draw needn't show every extreme that they name: `routes`: A token's two memories differ. Among the tokens of one device (an aligned block of 128 tokens) no memory is named by more than 40 tokens, and in some such block a memory is named by exactly 40. `log_decay`: entries are negative.
All inputs are finite; a program needn't handle non-finite values.
Results may differ from the reference program's by a relative error of at most 0.015.
Values may be sent and summed in bfloat16 or wider, within the bound.
A program may use at most 128 MiB of HBM per device.

```python
import math
import jax
import jax.numpy as jnp
import numpy as np
from jax import lax

HEAD_COUNT = 32
HD = 128
TOP = 2
TOK_DEV = 128
MEM = 8
CAP = 40
BLOCK_TOKENS = 1024
BLOCK_COUNT = 32
WINDOW_TOKENS = 32768
HH = 4096


def draw_log_decay(key, part):
    parallel_flows = jax.random.split(jax.random.fold_in(key, 11), 7)
    fast_count = HEAD_COUNT // 2
    order = jax.random.permutation(parallel_flows[0], HEAD_COUNT)
    gentle_decay = order >= fast_count
    slow_rate = jnp.exp(jax.random.uniform(parallel_flows[1], (HEAD_COUNT,), jnp.float32, math.log(0.1), math.log(0.8))) / (WINDOW_TOKENS // 2)
    fast_rate = jnp.exp(jax.random.uniform(parallel_flows[2], (HEAD_COUNT,), jnp.float32, math.log(0.05), math.log(0.08)))
    base = jnp.where(gentle_decay, slow_rate, fast_rate)
    block_factor = jnp.exp(jax.random.uniform(parallel_flows[3], (BLOCK_COUNT, 1, HEAD_COUNT), jnp.float32, math.log(0.6), math.log(1.6)))
    token_factor = jnp.exp(jax.random.uniform(parallel_flows[4], (BLOCK_COUNT, BLOCK_TOKENS, HEAD_COUNT), jnp.float32, math.log(0.5), math.log(1.5)))
    rate = base[None, None, :] * block_factor * token_factor
    spike_position = jax.random.randint(parallel_flows[5], (3,), 0, WINDOW_TOKENS)
    token_offsets = jnp.arange(WINDOW_TOKENS).reshape(BLOCK_COUNT, BLOCK_TOKENS)
    spike_active = jnp.any(token_offsets[:, :, None] == spike_position[None, None, :], axis=-1)
    spike_length = jax.random.uniform(parallel_flows[6], (BLOCK_COUNT, BLOCK_TOKENS, HEAD_COUNT), jnp.float32, math.log(0.5), math.log(0.8))
    additional_term = jnp.where(spike_active[:, :, None] & gentle_decay[None, None, :], spike_length, 0.0)
    return (additional_term - rate).astype(jnp.bfloat16)


def shard_levels(stream_key, shape, pieces, least, largest):
    factor_of = 1.0
    for axis_at, shards_of in pieces:
        draws = jax.random.uniform(jax.random.fold_in(jax.random.fold_in(stream_key, 6), axis_at), (shards_of,), jnp.float32, least / len(pieces), largest / len(pieces))
        factor_of = factor_of * jnp.repeat(jnp.exp(draws), shape[axis_at] // shards_of).reshape((-1,) + (1,) * (len(shape) - 1 - axis_at))
    return factor_of


def routed_block(stream_key, own, number, rows, amount, top, reach, slope):
    ranking = jax.random.permutation(stream_key, amount)
    crowded, usual = portions_of(amount, rows * top, reach, slope, True), portions_of(amount, rows * top, reach, slope, False)
    places = jnp.arange(amount)

    def named(lengths, offset_by):
        used = int((lengths > 0).sum())
        fixed = max(1, used // 4)
        moved = fixed + (places - fixed + offset_by * (used - fixed)) % max(1, amount - fixed)
        return jnp.zeros((amount,), jnp.int32).at[ranking[jnp.where(places < fixed, places, moved)]].set(jnp.asarray(lengths, jnp.int32))

    lengths = jnp.where(number % 4 == 0, named(crowded, number // 4), named(usual, number - number // 4 - 1))
    mixed = jax.random.permutation(jax.random.fold_in(own, 3), amount)
    giver, sink = mixed[0:amount // 2 * 2:2], mixed[1:amount // 2 * 2:2]
    margin = jnp.minimum(lengths[giver] - 1, reach - lengths[sink]) // 2
    margin = jnp.where((giver == ranking[0]) | (sink == ranking[0]) | (lengths[sink] == 0), 0, jnp.maximum(margin, 0))
    moved = jax.random.randint(jax.random.fold_in(own, 4), (amount // 2,), 0, 1 << 20) % (margin + 1)
    lengths = lengths.at[giver].add(-moved).at[sink].add(moved)
    members = jnp.searchsorted(jnp.cumsum(lengths), jnp.arange(rows * top), side="right").astype(jnp.int32)
    listing = members.reshape(top, rows).T
    listing = listing[jax.random.permutation(jax.random.fold_in(own, 1), rows)]
    offset_by = jax.random.randint(jax.random.fold_in(own, 2), (rows, 1), 0, top)
    return jnp.take_along_axis(listing, (jnp.arange(top)[None, :] + offset_by) % top, axis=1)


def portions_of(number_of, total, reach, slope, full):
    weights = [(1 << 20) // math.isqrt(grade ** slope) + 1 for grade in range(1, number_of + 1)]
    largest = reach if full else min(reach, max(-(-total // number_of), total * weights[0] // sum(weights)))
    least = 1 if total - largest >= number_of - 1 else 0
    holding, rest = [largest] + [least] * (number_of - 1), total - largest - least * (number_of - 1)
    while rest > 0:
        free = [i for i in range(1, number_of) if holding[i] < largest] or [i for i in range(1, number_of) if holding[i] < reach]
        pool, remaining = sum([weights[i] for i in free]), rest
        for i in free:
            addition = min(reach - holding[i], max(1, remaining * weights[i] // pool), rest)
            holding[i] = holding[i] + addition
            rest = rest - addition
    return np.array(holding)


def centred(own_key, extent, width, bound, shards=(), kind=jnp.bfloat16):
    factor_of = shard_levels(own_key, extent, shards, -0.22, 0.18) if shards else 1.0
    values = jax.random.normal(own_key, extent, jnp.float32) * width * factor_of
    return jnp.minimum(jnp.maximum(values, -bound), bound).astype(kind)


def setup_inputs(seed: int = 0) -> dict:
    arg_keys = jax.random.split(jax.random.key(seed), 8)
    queries = centred(arg_keys[0], (BLOCK_COUNT, BLOCK_TOKENS, HEAD_COUNT, HD), 1.0, 6.0, ((0, 32), (1, 8)))
    keys = centred(arg_keys[1], (BLOCK_COUNT, BLOCK_TOKENS, HEAD_COUNT, HD), 1.0, 6.0, ((0, 32), (1, 8)))
    values = centred(arg_keys[2], (BLOCK_COUNT, BLOCK_TOKENS, HEAD_COUNT, HD), 1.0, 6.0, ((0, 32), (1, 8)))
    log_decay = draw_log_decay(jax.random.fold_in(arg_keys[7], 71), 0)
    routes_keys = jax.random.split(jax.random.fold_in(arg_keys[4], 1), BLOCK_COUNT * BLOCK_TOKENS // TOK_DEV)
    routes_turns = jax.random.permutation(jax.random.fold_in(arg_keys[4], 3), BLOCK_COUNT * BLOCK_TOKENS // TOK_DEV)
    routes = jax.vmap(lambda own, number: routed_block(jax.random.fold_in(arg_keys[4], 2), own, number, TOK_DEV, MEM, TOP, CAP, 2))(routes_keys, routes_turns).reshape((BLOCK_COUNT, BLOCK_TOKENS, TOP))
    route_weight = jnp.clip(0.2 + 0.8 * jax.random.uniform(arg_keys[5], (BLOCK_COUNT, BLOCK_TOKENS, TOP), jnp.float32) ** shard_levels(arg_keys[5], (BLOCK_COUNT, BLOCK_TOKENS, TOP), ((0, 32), (1, 8)), -0.2, 0.2), 0.2, 1.0)
    gain = jnp.clip(1.0 + 0.15 * jax.random.normal(arg_keys[6], (HH,), jnp.float32), 0.25, 1.75)
    return dict(queries=queries, keys=keys, values=values, log_decay=log_decay, routes=routes, route_weight=route_weight, gain=gain)


def block_output(query_block_rows, key_block_rows, value_block_rows, block_rate, entering_state, query_scale):
    running_decay = jnp.cumsum(block_rate.astype(jnp.float32), axis=0)
    head_cumul = running_decay.T
    diff = head_cumul[:, :, None] - head_cumul[:, None, :]
    count_rows = query_block_rows.shape[0]
    causal = jnp.arange(count_rows)[:, None] >= jnp.arange(count_rows)[None, :]
    scores = jnp.einsum('ihd,jhd->hij', query_block_rows.astype(jnp.float32), key_block_rows.astype(jnp.float32), precision=lax.Precision.HIGHEST)
    weights = (jnp.where(causal, jnp.exp(jnp.where(causal, diff, 0.0)), 0.0) * scores * query_scale).astype(jnp.bfloat16)
    intra = jnp.einsum('hij,jhd->ihd', weights.astype(jnp.float32), value_block_rows.astype(jnp.float32), precision=lax.Precision.HIGHEST)
    across_block_output = jnp.einsum('epm,pmx->epx', query_block_rows.astype(jnp.float32), entering_state, precision=lax.Precision.HIGHEST) * (jnp.exp(running_decay) * query_scale)[:, :, None]
    readout = (intra + across_block_output).astype(jnp.bfloat16)
    total = running_decay[-1]
    retained_mask = jnp.exp(total[None, :] - running_decay)
    state_increment = jnp.einsum('dyn,dye->yne', key_block_rows.astype(jnp.float32) * retained_mask[:, :, None], value_block_rows.astype(jnp.float32), precision=lax.Precision.HIGHEST)
    state_out = jnp.exp(total)[:, None, None] * entering_state + state_increment
    return (readout, state_out)

def head_norm(rows):
    square_mean = lax.optimization_barrier(jnp.mean(rows * rows, axis=-1, keepdims=True))
    return rows * lax.rsqrt(square_mean + 1e-06)

def reference(queries, keys, values, log_decay, routes, route_weight, gain):
    slots = MEM * CAP
    query_scale = HD ** (-0.5)
    slot_ids = jnp.arange(slots, dtype=jnp.int32)
    token_offsets = jnp.arange(BLOCK_TOKENS, dtype=jnp.int32)
    gain_heads = gain.reshape(HEAD_COUNT, HD).astype(jnp.float32)

    def one_block(states, block):
        query_block_rows, key_block_rows, value_block_rows, block_rate, block_route, block_weight = block

        def one_memory(memory):
            named = block_route == memory
            member = jnp.any(named, axis=1)
            counted = member.astype(jnp.int32)
            rank = jnp.cumsum(counted) - counted
            match = member[None, :] & (rank[None, :] == slot_ids[:, None])
            source = lax.optimization_barrier(jnp.sum(jnp.where(match, token_offsets[None, :], 0), axis=1)).astype(jnp.int32)
            filled = jnp.any(match, axis=1)

            def packed(table):
                shaped = filled.reshape((-1,) + (1,) * (table.ndim - 1))
                return jnp.where(shaped, table[source], jnp.zeros((), table.dtype))
            readout, new_state = block_output(packed(query_block_rows), packed(key_block_rows), packed(value_block_rows), packed(block_rate), states[memory], query_scale)
            token_out = head_norm(readout[jnp.minimum(rank, slots - 1).astype(jnp.int32)].astype(jnp.float32))
            weight = lax.optimization_barrier(jnp.sum(jnp.where(named, block_weight, 0.0), axis=1))
            term = jnp.where(member[:, None, None], token_out, 0.0) * weight[:, None, None]
            return (term, new_state)
        terms, new_states = lax.map(one_memory, jnp.arange(MEM, dtype=jnp.int32))
        mixed = lax.optimization_barrier(jnp.sum(terms, axis=0))
        return (new_states, (mixed * gain_heads).astype(jnp.bfloat16))
    initial = jnp.zeros((MEM, HEAD_COUNT, HD, HD), jnp.float32)
    final_states, outputs = lax.scan(one_block, initial, (queries, keys, values, log_decay, routes, route_weight))
    return outputs
```

```python
import functools

import jax
import jax.numpy as jnp
from jax import lax
from jax.experimental import pallas as pl
from jax.experimental.pallas import tpu as pltpu
from jax.sharding import Mesh
from jax.sharding import PartitionSpec as P

GROUP = ("ctx_1", "mem_0", "mem_1")
SCAN = "ctx_0"
HEADS = 32
HD = 128
TOK = 128
MEM = 8
META = 16
PAIR = 2 * TOK
TILES = HEADS // 2
BF = jnp.bfloat16
F32 = jnp.float32
LIMIT = 56 * 1024 * 1024


def dot(a, b):
    return jnp.dot(a, b, preferred_element_type=F32)


def vmem_call(kernel, outs, scratch=()):
    return pl.pallas_call(
        kernel,
        out_shape=outs,
        scratch_shapes=list(scratch),
        compiler_params=pltpu.CompilerParams(vmem_limit_bytes=LIMIT),
    )


def pack_kernel(q_ref, k_ref, v_ref, meta_ref, qt_ref, kp_ref, vt_ref, flat):
    for source, dest, turned in ((k_ref, kp_ref, False), (v_ref, vt_ref, True), (q_ref, qt_ref, True)):
        flat[...] = source[...].astype(F32).reshape(TOK * HEADS, HD)

        def one(h, _):
            slab = flat[pl.ds(h, TOK, stride=HEADS), :]
            if turned:
                slab = slab.T
            dest[h, 0:TOK, :] = slab.astype(BF)
            return 0

        lax.fori_loop(0, HEADS, one, 0)
    kp_ref[:, TOK:, :] = meta_ref[...]


def pack(q, k, v, meta):
    slab = jax.ShapeDtypeStruct((HEADS, TOK, HD), BF)
    return vmem_call(
        pack_kernel,
        (slab, jax.ShapeDtypeStruct((HEADS, TOK + META, HD), BF), slab),
        [pltpu.VMEM((TOK * HEADS, HD), F32)],
    )(q, k, v, meta)


def unpack_kernel(got_ref, out_ref, flat):
    def one(h, _):
        flat[pl.ds(h, TOK, stride=HEADS), :] = got_ref[h].astype(F32)
        return 0

    lax.fori_loop(0, HEADS, one, 0)
    out_ref[...] = flat[...].astype(BF).reshape(TOK, HEADS, HD)


def unpack(got):
    return vmem_call(
        unpack_kernel,
        jax.ShapeDtypeStruct((TOK, HEADS, HD), BF),
        [pltpu.VMEM((TOK * HEADS, HD), F32)],
    )(got)


def tile_meta(kp_ref, c):
    first = kp_ref[2 * c, TOK : TOK + META, :].astype(F32)
    second = kp_ref[2 * c + 1, TOK : TOK + META, :].astype(F32)
    return jnp.concatenate([first, second], axis=1)


def tile_masks(meta):
    ids = lax.broadcasted_iota(jnp.int32, (MEM, PAIR), 0).astype(F32)
    oh0 = jnp.where(meta[1:2, :] == ids, 1.0, 0.0)
    oh1 = jnp.where(meta[2:3, :] == ids, 1.0, 0.0)
    return oh0, oh1


def running_decays(kp_ref, rates, sums):
    def one(c, _):
        meta = tile_meta(kp_ref, c)
        oh0, oh1 = tile_masks(meta)
        rates[pl.ds(c * MEM, MEM), :] = (oh0 + oh1) * meta[0:1, :]
        return 0

    lax.fori_loop(0, TILES, one, 0)
    before = lax.broadcasted_iota(jnp.int32, (PAIR, PAIR), 0)
    after = lax.broadcasted_iota(jnp.int32, (PAIR, PAIR), 1)
    upper = jnp.where(before <= after, 1.0, 0.0).astype(BF)
    sums[...] = dot(rates[...].astype(BF), upper)


def pair(ref, c):
    return jnp.concatenate([ref[2 * c], ref[2 * c + 1]], axis=1)


def pair_keys(kp_ref, c):
    return jnp.concatenate([kp_ref[2 * c, 0:TOK, :], kp_ref[2 * c + 1, 0:TOK, :]], axis=0)


def tile_increment(vt, keys, mask, run):
    total = run[:, PAIR - 1 : PAIR]
    kept = mask * jnp.exp(total - run)
    wide = vt.astype(F32)
    scaled = jnp.concatenate([(wide * kept[m : m + 1, :]).astype(BF) for m in range(MEM)], axis=0)
    return dot(scaled, keys)


def advance(state, inc, total):
    gone = jnp.exp(total)
    for m in range(MEM):
        cols = slice(m * HD, (m + 1) * HD)
        state[:, cols] = state[:, cols] * gone[m : m + 1, :] + inc[cols, :]


def state_kernel(kp_ref, vt_ref, out_ref, rates, sums, state):
    running_decays(kp_ref, rates, sums)
    state[...] = jnp.zeros_like(state)

    def one(c, whole):
        oh0, oh1 = tile_masks(tile_meta(kp_ref, c))
        run = sums[pl.ds(c * MEM, MEM), :]
        inc = tile_increment(pair(vt_ref, c), pair_keys(kp_ref, c), oh0 + oh1, run)
        total = run[:, PAIR - 1 : PAIR]
        advance(state, inc, total)
        return whole + total

    whole = lax.fori_loop(0, TILES, one, jnp.zeros((MEM, 1), F32))
    left = jnp.exp(whole)
    high = left.astype(BF).astype(F32)
    low = left - high
    row = lax.broadcasted_iota(jnp.int32, (META, HD), 0)
    for m in range(MEM):
        out_ref[m, 0:HD, :] = state[:, m * HD : (m + 1) * HD].astype(BF)
        out_ref[m, HD:, :] = jnp.where(row == 0, high[m : m + 1, :], low[m : m + 1, :]).astype(BF)


def tile_scratch():
    return [
        pltpu.VMEM((TILES * MEM, PAIR), F32),
        pltpu.VMEM((TILES * MEM, PAIR), F32),
        pltpu.VMEM((HD, MEM * HD), F32),
    ]


def chunk_state(kp, vt):
    return vmem_call(
        state_kernel, jax.ShapeDtypeStruct((MEM, HD + META, HD), BF), tile_scratch()
    )(kp, vt)


def compose_kernel(parts_ref, out_ref):
    run = jnp.zeros((HD, HD), F32)
    for z in range(parts_ref.shape[0]):
        out_ref[z] = run.astype(BF)
        left = parts_ref[z, HD : HD + META, :].astype(F32)
        run = run * (left[0:1, :] + left[1:2, :]) + parts_ref[z, 0:HD, :].astype(F32)


def compose(parts):
    return vmem_call(compose_kernel, jax.ShapeDtypeStruct((parts.shape[0], HD, HD), BF))(parts)


def split_rows(rows):
    high = rows.astype(BF).astype(F32)
    return high, rows - high


def read_kernel(kp_ref, vt_ref, qt_ref, enter_ref, gain_ref, out_ref, rates, sums, state):
    scale = HD**-0.5
    running_decays(kp_ref, rates, sums)
    for m in range(MEM):
        state[:, m * HD : (m + 1) * HD] = enter_ref[m].astype(F32)
    gain = gain_ref[...]
    earlier = lax.broadcasted_iota(jnp.int32, (PAIR, PAIR), 0)
    later = lax.broadcasted_iota(jnp.int32, (PAIR, PAIR), 1)
    causal = earlier <= later

    def one(c, _):
        meta = tile_meta(kp_ref, c)
        oh0, oh1 = tile_masks(meta)
        mask = oh0 + oh1
        run = sums[pl.ds(c * MEM, MEM), :]
        total = run[:, PAIR - 1 : PAIR]
        middle = 0.5 * total
        up = jnp.exp(run - middle) * scale
        down_h, down_l = split_rows(mask * jnp.exp(middle - run))
        below = jnp.concatenate([down_h, down_l, down_h, down_l], axis=0).astype(BF)
        vt, keys, qt = pair(vt_ref, c), pair_keys(kp_ref, c), pair(qt_ref, c)
        scores = dot(keys, qt)
        old = state[...].astype(BF)
        reach = jnp.exp(run) * scale
        mixed = jnp.zeros((HD, PAIR), F32)
        grouped = qt.reshape(HD // 16, 16, PAIR)
        for oh, high_row in ((oh0, 3), (oh1, 5)):
            up_h, up_l = split_rows(oh * up)
            above = jnp.concatenate([up_h, up_h, up_l, up_l], axis=0).astype(BF)
            decay = lax.dot_general(
                below, above, (((0,), (0,)), ((), ())), preferred_element_type=F32
            )
            weights = jnp.where(causal, scores * decay, 0.0).astype(BF)
            inside = dot(vt, weights)
            chosen = jnp.concatenate(
                [
                    (
                        grouped * jnp.broadcast_to(oh[m : m + 1, :], (16, PAIR)).astype(BF)[None]
                    ).reshape(HD, PAIR)
                    for m in range(MEM)
                ],
                axis=0,
            )
            across = dot(old, chosen)
            full = inside + across * jnp.sum(oh * reach, axis=0, keepdims=True)
            square = jnp.mean(full * full, axis=0, keepdims=True)
            weight = meta[high_row : high_row + 1, :] + meta[high_row + 1 : high_row + 2, :]
            mixed = mixed + full * (lax.rsqrt(square + 1e-06) * weight)
        mixed = (mixed * gain).T.astype(BF)
        out_ref[2 * c] = mixed[0:TOK]
        out_ref[2 * c + 1] = mixed[TOK:]
        advance(state, tile_increment(vt, keys, mask, run), total)
        return 0

    lax.fori_loop(0, TILES, one, 0)


def read(kp, vt, qt, enter, gain):
    return vmem_call(
        read_kernel, jax.ShapeDtypeStruct((HEADS, TOK, HD), BF), tile_scratch()
    )(kp, vt, qt, enter, gain)


def make_meta(log_decay, routes, route_weight):
    high = route_weight.astype(BF)
    low = (route_weight - high.astype(F32)).astype(BF)
    named = routes.astype(BF)
    common = jnp.stack([named[:, 0], named[:, 1], high[:, 0], low[:, 0], high[:, 1], low[:, 1]])
    common = jnp.pad(common, ((0, META - 7), (0, 0)))
    common = jnp.broadcast_to(common[None], (HEADS, META - 1, TOK))
    return jnp.concatenate([log_decay.T[:, None, :], common], axis=1)


def exchange(parts, axes):
    return lax.all_to_all(parts, axes, split_axis=0, concat_axis=0, tiled=True)


def shards(queries, keys, values, log_decay, routes, route_weight, gain):
    meta = make_meta(log_decay[0], routes[0], route_weight[0])
    qt, kp, vt = pack(queries[0], keys[0], values[0], meta)
    kp = exchange(kp, GROUP)
    vt = exchange(vt, GROUP)
    qt = exchange(qt, GROUP)
    mine = chunk_state(kp, vt)
    enter = exchange(compose(exchange(mine, SCAN)), SCAN)
    own = lax.dynamic_slice_in_dim(gain, lax.axis_index(GROUP) * HD, HD)[:, None]
    done = read(kp, vt, qt, enter, own)
    return unpack(exchange(done, GROUP))[None]


def solution(mesh):
    finer = Mesh(mesh.devices.reshape(4, 2, 8, 4), ("mem_0", "mem_1", "ctx_0", "ctx_1"))
    ctx = ("ctx_0", "ctx_1")
    mem = ("mem_0", "mem_1")
    return jax.shard_map(
        shards,
        mesh=finer,
        in_specs=(
            P(ctx, mem, None, None),
            P(ctx, mem, None, None),
            P(ctx, mem, None, None),
            P(ctx, mem, None),
            P(ctx, mem, None),
            P(ctx, mem, None),
            P(),
        ),
        out_specs=P(ctx, mem, None, None),
        check_vma=False,
    )
```

```python
import jax
import jax.numpy as jnp
from jax import lax
from jax.experimental import pallas as pl
from jax.experimental.pallas import tpu as pltpu
from jax.sharding import Mesh
from jax.sharding import PartitionSpec as P

HEADS = 32
HD = 128
TOK = 128
MEM = 8
META = 16
PAIR = 2 * TOK
TILES = HEADS // 2
SLAB = TOK + META + HD
BF = jnp.bfloat16
F32 = jnp.float32
SCALE = HD**-0.5
MESH = pl.DeviceIdType.MESH


def dot(a, b):
    return jnp.dot(a, b, preferred_element_type=F32)


class Place:
    def __init__(self):
        self.x, self.y = lax.axis_index("ctx_1"), lax.axis_index("mem_0")
        self.c, self.z = lax.axis_index("mem_1"), lax.axis_index("ctx_0")
        self.me = (self.x * 4 + self.y) * 2 + self.c

    def target(self, chip, core):
        x, y = lax.rem(self.x + chip // 4, 4), lax.rem(self.y + lax.rem(chip, 4), 4)
        c = lax.rem(self.c + core, 2)
        return x * 4 + y, (x * 4 + y) * 2 + c, {"ctx_1": x, "mem_0": y, "mem_1": c}

    def source(self, chip, core):
        x = lax.rem(self.x + 4 - chip // 4, 4)
        y = lax.rem(self.y + 4 - lax.rem(chip, 4), 4)
        c = lax.rem(self.c + core, 2)
        return x * 4 + y, (x * 4 + y) * 2 + c

    def along(self, off):
        to = lax.rem(self.z + off, 8)
        return to, {"ctx_0": to}

    def back(self, off):
        return lax.rem(self.z + 8 - off, 8)


def remote(src, dst, sems, slot, device):
    return pltpu.make_async_remote_copy(
        src_ref=src,
        dst_ref=dst,
        send_sem=sems[0].at[slot],
        recv_sem=sems[1].at[slot],
        device_id=device,
        device_id_type=MESH,
    )


def loop(lo, hi, body):
    def step(i, _):
        body(i)
        return 0

    lax.fori_loop(lo, hi, step, 0)


def tile_meta(got, c):
    first = got[2 * c, TOK : TOK + META, :].astype(F32)
    second = got[2 * c + 1, TOK : TOK + META, :].astype(F32)
    return jnp.concatenate([first, second], axis=1)


def tile_masks(meta):
    ids = lax.broadcasted_iota(jnp.int32, (MEM, PAIR), 0).astype(F32)
    return jnp.where(meta[1:2, :] == ids, 1.0, 0.0), jnp.where(meta[2:3, :] == ids, 1.0, 0.0)


def pair_keys(got, c):
    return jnp.concatenate([got[2 * c, 0:TOK, :], got[2 * c + 1, 0:TOK, :]], axis=0)


def pair_values(got, c):
    return jnp.concatenate([got[2 * c, TOK + META :, :], got[2 * c + 1, TOK + META :, :]], axis=1)


def split_rows(rows):
    high = rows.astype(BF).astype(F32)
    return high, rows - high


def chosen_queries(qt, oh):
    grouped = qt.reshape(HD // 16, 16, PAIR)
    parts = []
    for m in range(MEM):
        row = jnp.broadcast_to(oh[m : m + 1, :], (16, PAIR)).astype(BF)
        parts.append((grouped * row[None]).reshape(HD, PAIR))
    return jnp.concatenate(parts, axis=0)


def layer_kernel(
    q_ref,
    k_ref,
    v_ref,
    rate_ref,
    route_ref,
    weight_ref,
    gain_ref,
    out_ref,
    flat_a,
    flat_b,
    rates,
    slabs,
    got,
    q_out,
    q_got,
    o_out,
    o_got,
    z_out,
    z_got,
    e_out,
    e_got,
    enter,
    sums,
    bases,
    incs,
    locals_,
    parts,
    state,
    kv_s,
    kv_r,
    q_s,
    q_r,
    o_s,
    o_r,
    z_s,
    z_r,
    e_s,
    e_r,
):
    at = Place()
    me = at.me
    kv_sem, q_sem, o_sem, z_sem, e_sem = (kv_s, kv_r), (q_s, q_r), (o_s, o_r), (z_s, z_r), (e_s, e_r)

    barrier = pltpu.get_barrier_semaphore()

    def greet(device):
        pl.semaphore_signal(barrier, inc=1, device_id=device, device_id_type=MESH)

    greet(at.target(0, 1)[2])
    loop(1, TILES, lambda t: [greet(at.target(t, core)[2]) for core in (0, 1)])
    loop(1, 8, lambda off: greet(at.along(off)[1]))

    flat_a[...] = k_ref[...].astype(F32).reshape(TOK * HEADS, HD)
    flat_b[...] = v_ref[...].astype(F32).reshape(TOK * HEADS, HD)
    rates[...] = rate_ref[...].astype(F32)
    row = lax.broadcasted_iota(jnp.int32, (META, TOK), 0)
    named = route_ref[...].astype(F32)
    high, low = split_rows(weight_ref[...])
    common = jnp.zeros((META, TOK), F32)
    lines = (named[0:1], named[1:2], high[0:1], low[0:1], high[1:2], low[1:2])
    for i, line in enumerate(lines):
        common = jnp.where(row == i + 1, line, common)

    pl.semaphore_wait(barrier, 38)

    def by_head(flat, d):
        return flat[pl.ds(d, TOK, stride=HEADS), :]

    def pack_kv(d, dest, slot):
        dest[slot, 0:TOK, :] = by_head(flat_a, d).astype(BF)
        dest[slot, TOK : TOK + META, :] = jnp.where(row == 0, rates[pl.ds(d, 1), :], common).astype(BF)
        dest[slot, TOK + META :, :] = by_head(flat_b, d).T.astype(BF)

    def kv_copy(chip, core):
        _, d, device = at.target(chip, core)
        return remote(slabs.at[d], got.at[me], kv_sem, 2 * chip + core, device)

    def send_kv(chip, core):
        d = at.target(chip, core)[1]
        pack_kv(d, slabs, d)
        kv_copy(chip, core).start()

    send_kv(0, 1)
    loop(1, TILES, lambda t: [send_kv(t, core) for core in (0, 1)])
    pack_kv(me, got, me)

    flat_a[...] = q_ref[...].astype(F32).reshape(TOK * HEADS, HD)

    def q_copy(chip, core):
        _, d, device = at.target(chip, core)
        return remote(q_out.at[d], q_got.at[me], q_sem, 2 * chip + core, device)

    def send_q(chip, core):
        d = at.target(chip, core)[1]
        q_out[d] = by_head(flat_a, d).T.astype(BF)
        q_copy(chip, core).start()

    send_q(0, 1)
    loop(1, TILES, lambda t: [send_q(t, core) for core in (0, 1)])
    q_got[me] = by_head(flat_a, me).T.astype(BF)

    first = lax.broadcasted_iota(jnp.int32, (PAIR, PAIR), 0)
    second = lax.broadcasted_iota(jnp.int32, (PAIR, PAIR), 1)
    causal = first <= second

    def gather_tile(c):
        meta = tile_meta(got, c)
        oh0, oh1 = tile_masks(meta)
        mask = oh0 + oh1
        upper = jnp.where(causal, 1.0, 0.0).astype(BF)
        run = dot((mask * meta[0:1, :]).astype(BF), upper)
        sums[pl.ds(c * MEM, MEM), :] = run
        kept = mask * jnp.exp(run[:, PAIR - 1 : PAIR] - run)
        wide = pair_values(got, c).astype(F32)
        scaled = jnp.concatenate(
            [(wide * kept[m : m + 1, :]).astype(BF) for m in range(MEM)], axis=0
        )
        incs[c] = dot(scaled, pair_keys(got, c))

    kv_copy(0, 1).wait_recv()
    gather_tile(at.source(0, 0)[0])

    def arrived(t):
        for core in (0, 1):
            kv_copy(t, core).wait_recv()
        gather_tile(at.source(t, 0)[0])

    loop(1, TILES, arrived)

    state[...] = jnp.zeros_like(state)

    def advance(c, base):
        locals_[c] = state[...].astype(BF)
        bases[pl.ds(c * MEM, MEM), :] = jnp.broadcast_to(base, (MEM, HD))
        total = sums[pl.ds(c * MEM, MEM), :][:, PAIR - 1 : PAIR]
        gone = jnp.exp(total)
        for m in range(MEM):
            cols = slice(m * HD, (m + 1) * HD)
            state[:, cols] = state[:, cols] * gone[m : m + 1, :] + incs[c, cols, :]
        return base + total

    whole = lax.fori_loop(0, TILES, advance, jnp.zeros((MEM, 1), F32))
    left_h, left_l = split_rows(jnp.exp(whole))
    for m in range(MEM):
        z_out[m, 0:HD, :] = state[:, m * HD : (m + 1) * HD].astype(BF)
        z_out[m, HD:, :] = jnp.where(row == 0, left_h[m : m + 1, :], left_l[m : m + 1, :]).astype(BF)

    def z_copy(off):
        to, device = at.along(off)
        return remote(z_out.at[to], z_got.at[at.z], z_sem, off, device)

    loop(1, 8, lambda off: z_copy(off).start())
    z_got[at.z] = z_out[at.z]

    def inside_tile(c):
        meta = tile_meta(got, c)
        oh0, oh1 = tile_masks(meta)
        run = sums[pl.ds(c * MEM, MEM), :]
        middle = 0.5 * run[:, PAIR - 1 : PAIR]
        up = jnp.exp(run - middle) * SCALE
        down_h, down_l = split_rows((oh0 + oh1) * jnp.exp(middle - run))
        below = jnp.concatenate([down_h, down_l, down_h, down_l], axis=0).astype(BF)
        vt = pair_values(got, c)
        qt = jnp.concatenate([q_got[2 * c], q_got[2 * c + 1]], axis=1)
        scores = dot(pair_keys(got, c), qt)
        reach = jnp.exp(run) * SCALE
        for j, oh in enumerate((oh0, oh1)):
            up_h, up_l = split_rows(oh * up)
            above = jnp.concatenate([up_h, up_h, up_l, up_l], axis=0).astype(BF)
            decay = lax.dot_general(
                below, above, (((0,), (0,)), ((), ())), preferred_element_type=F32
            )
            weights = jnp.where(causal, scores * decay, 0.0).astype(BF)
            across = dot(locals_[c], chosen_queries(qt, oh))
            parts[c, j] = dot(vt, weights) + across * jnp.sum(oh * reach, axis=0, keepdims=True)

    def inside(t):
        for core in (0, 1):
            q_copy(t, core).wait_recv()
        inside_tile(at.source(t, 0)[0])

    q_copy(0, 1).wait_recv()
    inside_tile(at.source(0, 0)[0])
    loop(1, TILES // 2, inside)

    loop(1, 8, lambda off: z_copy(off).wait_recv())
    entering = jnp.zeros((HD, HD), F32)
    for z in range(8):
        e_out[z] = entering.astype(BF)
        left = z_got[z, HD : HD + META, :].astype(F32)
        entering = entering * (left[0:1, :] + left[1:2, :]) + z_got[z, 0:HD, :].astype(F32)

    def e_copy(off):
        to, device = at.along(off)
        return remote(e_out.at[to], e_got.at[at.z], e_sem, off, device)

    loop(1, 8, lambda off: e_copy(off).start())
    e_got[at.z] = e_out[at.z]

    loop(TILES // 2, TILES, inside)

    loop(1, 8, lambda off: e_copy(off).wait_recv())
    for m in range(MEM):
        enter[:, m * HD : (m + 1) * HD] = e_got[m]
    gain = gain_ref[pl.ds(me, 1), :]

    def finish_tile(c):
        meta = tile_meta(got, c)
        qt = jnp.concatenate([q_got[2 * c], q_got[2 * c + 1]], axis=1)
        base = bases[pl.ds(c * MEM, MEM), :][:, 0:1]
        reach = jnp.exp(sums[pl.ds(c * MEM, MEM), :] + base) * SCALE
        mixed = jnp.zeros((HD, PAIR), F32)
        for j, oh in enumerate(tile_masks(meta)):
            across = dot(enter[...], chosen_queries(qt, oh))
            full = parts[c, j] + across * jnp.sum(oh * reach, axis=0, keepdims=True)
            square = jnp.mean(full * full, axis=0, keepdims=True)
            weight = meta[3 + 2 * j : 4 + 2 * j, :] + meta[4 + 2 * j : 5 + 2 * j, :]
            mixed = mixed + full * (lax.rsqrt(square + 1e-06) * weight)
        return (mixed.T * gain).astype(BF)

    def o_copy(chip, core):
        _, d, device = at.target(chip, core)
        return remote(o_out.at[d], o_got.at[me], o_sem, 2 * chip + core, device)

    def finish(t):
        c = at.target(t, 0)[0]
        done = finish_tile(c)
        o_out[2 * c] = done[0:TOK]
        o_out[2 * c + 1] = done[TOK:]
        for core in (0, 1):
            o_copy(t, core).start()

    loop(1, TILES, finish)
    home = at.target(0, 0)[0]
    done = finish_tile(home)
    o_out[2 * home] = done[0:TOK]
    o_out[2 * home + 1] = done[TOK:]
    o_copy(0, 1).start()
    o_got[me] = o_out[me]

    def unpack(s):
        out_ref[pl.ds(s, TOK, stride=HEADS), :] = o_got[s].astype(F32)

    def returned(t):
        for core in (0, 1):
            o_copy(t, core).wait_recv()
            unpack(at.source(t, core)[1])

    loop(1, TILES, returned)
    o_copy(0, 1).wait_recv()
    unpack(at.source(0, 1)[1])
    unpack(me)

    for copy in (kv_copy, q_copy, o_copy):
        copy(0, 1).wait_send()
        loop(1, TILES, lambda t, copy=copy: [copy(t, core).wait_send() for core in (0, 1)])
    for copy in (z_copy, e_copy):
        loop(1, 8, lambda off, copy=copy: copy(off).wait_send())


def shards(queries, keys, values, log_decay, routes, route_weight, gain):
    sems = [pltpu.SemaphoreType.DMA((HEADS,))] * 6 + [pltpu.SemaphoreType.DMA((8,))] * 4
    out = pl.pallas_call(
        layer_kernel,
        out_shape=jax.ShapeDtypeStruct((TOK * HEADS, HD), F32),
        in_specs=[pl.BlockSpec(memory_space=pltpu.VMEM)] * 7,
        out_specs=pl.BlockSpec(memory_space=pltpu.VMEM),
        scratch_shapes=[
            pltpu.VMEM((TOK * HEADS, HD), F32),
            pltpu.VMEM((TOK * HEADS, HD), F32),
            pltpu.VMEM((HEADS, TOK), F32),
            pltpu.VMEM((HEADS, SLAB, HD), BF),
            pltpu.VMEM((HEADS, SLAB, HD), BF),
            pltpu.VMEM((HEADS, HD, TOK), BF),
            pltpu.VMEM((HEADS, HD, TOK), BF),
            pltpu.VMEM((HEADS, TOK, HD), BF),
            pltpu.VMEM((HEADS, TOK, HD), BF),
            pltpu.VMEM((MEM, HD + META, HD), BF),
            pltpu.VMEM((MEM, HD + META, HD), BF),
            pltpu.VMEM((8, HD, HD), BF),
            pltpu.VMEM((8, HD, HD), BF),
            pltpu.VMEM((HD, MEM * HD), BF),
            pltpu.VMEM((TILES * MEM, PAIR), F32),
            pltpu.VMEM((TILES * MEM, HD), F32),
            pltpu.VMEM((TILES, MEM * HD, HD), F32),
            pltpu.VMEM((TILES, HD, MEM * HD), BF),
            pltpu.VMEM((TILES, 2, HD, PAIR), F32),
            pltpu.VMEM((HD, MEM * HD), F32),
            *sems,
        ],
        compiler_params=pltpu.CompilerParams(
            collective_id=0, has_side_effects=True, vmem_limit_bytes=50 * 1024 * 1024
        ),
        cost_estimate=pl.CostEstimate(
            flops=8 * 10**9, bytes_accessed=6 * 2**20, transcendentals=10**6
        ),
    )(
        queries[0],
        keys[0],
        values[0],
        log_decay[0].T,
        routes[0].T,
        route_weight[0].T,
        gain.reshape(HEADS, HD),
    )
    return out.astype(BF).reshape(1, TOK, HEADS, HD)


def solution(mesh):
    finer = Mesh(mesh.devices.reshape(4, 2, 8, 4), ("mem_0", "mem_1", "ctx_0", "ctx_1"))
    ctx = ("ctx_0", "ctx_1")
    mem = ("mem_0", "mem_1")
    return jax.shard_map(
        shards,
        mesh=finer,
        in_specs=(
            P(ctx, mem, None, None),
            P(ctx, mem, None, None),
            P(ctx, mem, None, None),
            P(ctx, mem, None),
            P(ctx, mem, None),
            P(ctx, mem, None),
            P(),
        ),
        out_specs=P(ctx, mem, None, None),
        check_vma=False,
    )
```

```python
import jax
import jax.numpy as jnp
from jax import lax
from jax.experimental import pallas as pl
from jax.experimental.pallas import tpu as pltpu
from jax.sharding import Mesh
from jax.sharding import PartitionSpec as P

HEADS = 32
HD = 128
TOK = 128
MEM = 8
META = 16
PAIR = 2 * TOK
TILES = HEADS // 2
EARLY = 6
FIRST = 6
SLAB = TOK + META + HD
BF = jnp.bfloat16
F32 = jnp.float32
SCALE = HD**-0.5
MESH = pl.DeviceIdType.MESH


def dot(a, b):
    return jnp.dot(a, b, preferred_element_type=F32)


ORDER = (
    ((0, 0), (1, 3), (3, 1), (2, 2), (1, 1), (3, 3), (1, 2), (3, 2))
    + ((2, 1), (2, 3), (0, 1), (1, 0), (0, 3), (3, 0), (0, 2), (2, 0))
)


def coded(values):
    whole = sum(v << (2 * i) for i, v in enumerate(values))
    return whole - (1 << 32) if whole >= 1 << 31 else whole


STEP_X, STEP_Y = coded([a for a, _ in ORDER]), coded([b for _, b in ORDER])


def offset(chip):
    if isinstance(chip, int):
        return ORDER[chip]
    turn = 2 * chip
    return tuple(jnp.bitwise_and(jnp.right_shift(jnp.int32(w), turn), 3) for w in (STEP_X, STEP_Y))


class Place:
    def __init__(self):
        self.x, self.y = lax.axis_index("ctx_1"), lax.axis_index("mem_0")
        self.c, self.z = lax.axis_index("mem_1"), lax.axis_index("ctx_0")
        self.me = (self.x * 4 + self.y) * 2 + self.c

    def target(self, chip, core):
        dx, dy = offset(chip)
        x, y, c = lax.rem(self.x + dx, 4), lax.rem(self.y + dy, 4), lax.rem(self.c + core, 2)
        return x * 4 + y, (x * 4 + y) * 2 + c, {"ctx_1": x, "mem_0": y, "mem_1": c}

    def source(self, chip, core):
        dx, dy = offset(chip)
        x, y, c = lax.rem(self.x + 4 - dx, 4), lax.rem(self.y + 4 - dy, 4), lax.rem(self.c + core, 2)
        return x * 4 + y, (x * 4 + y) * 2 + c

    def along(self, off):
        to = lax.rem(self.z + off, 8)
        return to, {"ctx_0": to}

    def back(self, off):
        return lax.rem(self.z + 8 - off, 8)


def remote(src, dst, sems, slot, device):
    return pltpu.make_async_remote_copy(
        src_ref=src,
        dst_ref=dst,
        send_sem=sems[0].at[slot],
        recv_sem=sems[1].at[slot],
        device_id=device,
        device_id_type=MESH,
    )


def loop(lo, hi, body):
    def step(i, _):
        body(i)
        return 0

    lax.fori_loop(lo, hi, step, 0)


def tile_meta(got, c):
    first = got[2 * c, TOK : TOK + META, :].astype(F32)
    second = got[2 * c + 1, TOK : TOK + META, :].astype(F32)
    return jnp.concatenate([first, second], axis=1)


def tile_masks(meta):
    ids = lax.broadcasted_iota(jnp.int32, (MEM, PAIR), 0).astype(F32)
    return jnp.where(meta[1:2, :] == ids, 1.0, 0.0), jnp.where(meta[2:3, :] == ids, 1.0, 0.0)


def pair_keys(got, c):
    return jnp.concatenate([got[2 * c, 0:TOK, :], got[2 * c + 1, 0:TOK, :]], axis=0)


def pair_values(got, c):
    return jnp.concatenate([got[2 * c, TOK + META :, :], got[2 * c + 1, TOK + META :, :]], axis=1)


def split_rows(rows):
    high = rows.astype(BF).astype(F32)
    return high, rows - high


def side_by_side(states):
    return jnp.concatenate([states[m] for m in range(MEM)], axis=1)


def chosen_queries(qt, oh):
    grouped = qt.reshape(HD // 16, 16, PAIR)
    parts = []
    for m in range(MEM):
        row = jnp.broadcast_to(oh[m : m + 1, :], (16, PAIR)).astype(BF)
        parts.append((grouped * row[None]).reshape(HD, PAIR))
    return jnp.concatenate(parts, axis=0)


def layer_kernel(
    q_ref,
    k_ref,
    v_ref,
    rate_ref,
    route_ref,
    weight_ref,
    gain_ref,
    out_ref,
    q_here,
    k_here,
    v_here,
    rate_here,
    route_here,
    weight_here,
    gain_here,
    flat_a,
    flat_b,
    rates,
    slabs,
    got,
    q_out,
    q_got,
    o_out,
    o_got,
    z_out,
    z_got,
    e_out,
    e_got,
    left,
    totals,
    sums,
    bases,
    incs,
    locals_,
    parts,
    kv_s,
    kv_r,
    q_s,
    q_r,
    o_s,
    o_r,
    z_s,
    z_r,
    e_s,
    e_r,
    in_s,
):
    at = Place()
    me = at.me
    kv_sem, q_sem, o_sem, z_sem, e_sem = (kv_s, kv_r), (q_s, q_r), (o_s, o_r), (z_s, z_r), (e_s, e_r)

    fetches = [
        pltpu.make_async_copy(there, here, in_s.at[i])
        for i, (there, here) in enumerate(
            (
                (k_ref, k_here),
                (v_ref, v_here),
                (rate_ref, rate_here),
                (route_ref, route_here),
                (weight_ref, weight_here),
                (gain_ref, gain_here),
                (q_ref, q_here),
            )
        )
    ]
    for fetch in fetches:
        fetch.start()
    barrier = pltpu.get_barrier_semaphore()

    def greet(device):
        pl.semaphore_signal(barrier, inc=1, device_id=device, device_id_type=MESH)

    greet(at.target(0, 1)[2])
    loop(1, TILES, lambda t: [greet(at.target(t, core)[2]) for core in (0, 1)])
    loop(1, 8, lambda off: greet(at.along(off)[1]))

    fetches[0].wait()
    flat_a[...] = k_here[...].astype(F32).reshape(TOK * HEADS, HD)
    fetches[1].wait()
    flat_b[...] = v_here[...].astype(F32).reshape(TOK * HEADS, HD)
    for fetch in fetches[2:]:
        fetch.wait()
    rates[...] = rate_here[...].astype(F32)
    row = lax.broadcasted_iota(jnp.int32, (META, TOK), 0)
    named = route_here[...].astype(F32)
    high, low = split_rows(weight_here[...])
    common = jnp.zeros((META, TOK), F32)
    lines = (named[0:1], named[1:2], high[0:1], low[0:1], high[1:2], low[1:2])
    for i, line in enumerate(lines):
        common = jnp.where(row == i + 1, line, common)

    def by_head(flat, d):
        return flat[pl.ds(d, TOK, stride=HEADS), :]

    def pack_kv(d, dest, slot):
        dest[slot, 0:TOK, :] = by_head(flat_a, d).astype(BF)
        dest[slot, TOK : TOK + META, :] = jnp.where(row == 0, rates[pl.ds(d, 1), :], common).astype(BF)
        dest[slot, TOK + META :, :] = by_head(flat_b, d).T.astype(BF)

    def kv_copy(chip, core):
        _, d, device = at.target(chip, core)
        return remote(slabs.at[d], got.at[me], kv_sem, 2 * chip + core, device)

    def pack_pair(t):
        for core in (0, 1):
            d = at.target(t, core)[1]
            pack_kv(d, slabs, d)

    def start_pair(copy, t):
        for core in (0, 1):
            copy(t, core).start()

    loop(1, EARLY, pack_pair)
    pl.semaphore_wait(barrier, 38)
    loop(1, EARLY, lambda t: start_pair(kv_copy, t))

    def pack_and_start(t):
        pack_pair(t)
        start_pair(kv_copy, t)

    loop(EARLY, TILES, pack_and_start)
    sibling = at.target(0, 1)[1]
    pack_kv(sibling, slabs, sibling)
    kv_copy(0, 1).start()
    pack_kv(me, got, me)

    flat_a[...] = q_here[...].astype(F32).reshape(TOK * HEADS, HD)

    def q_copy(chip, core):
        _, d, device = at.target(chip, core)
        return remote(q_out.at[d], q_got.at[me], q_sem, 2 * chip + core, device)

    def pack_q(d, dest):
        dest[d] = by_head(flat_a, d).T.astype(BF)

    loop(1, TILES, lambda t: [pack_q(at.target(t, core)[1], q_out) for core in (0, 1)])
    pack_q(sibling, q_out)
    q_got[me] = by_head(flat_a, me).T.astype(BF)

    first = lax.broadcasted_iota(jnp.int32, (PAIR, PAIR), 0)
    second = lax.broadcasted_iota(jnp.int32, (PAIR, PAIR), 1)
    causal = first <= second

    def gather_tile(c):
        meta = tile_meta(got, c)
        oh0, oh1 = tile_masks(meta)
        mask = oh0 + oh1
        upper = jnp.where(causal, 1.0, 0.0).astype(BF)
        run = dot((mask * meta[0:1, :]).astype(BF), upper)
        sums[pl.ds(c * MEM, MEM), :] = run
        total = run[:, PAIR - 1 : PAIR]
        totals[pl.ds(c * MEM, MEM), :] = jnp.broadcast_to(total, (MEM, HD))
        kept = mask * jnp.exp(total - run)
        wide = pair_values(got, c).astype(F32)
        scaled = jnp.concatenate(
            [(wide * kept[m : m + 1, :]).astype(BF) for m in range(MEM)], axis=0
        )
        incs[c] = dot(scaled, pair_keys(got, c)).reshape(MEM, HD, HD)

    kv_copy(0, 1).wait_recv()
    gather_tile(at.source(0, 0)[0])

    def arrived(t):
        for core in (0, 1):
            kv_copy(t, core).wait_recv()
        gather_tile(at.source(t, 0)[0])

    loop(1, TILES, arrived)

    def add_total(c, base):
        at_c = pl.ds(c * MEM, MEM)
        total = totals[at_c, :]
        bases[at_c, :] = base
        totals[at_c, :] = jnp.exp(total)
        return base + total

    whole = lax.fori_loop(0, TILES, add_total, jnp.zeros((MEM, HD), F32))
    left_h, left_l = split_rows(jnp.exp(whole))
    left[0:MEM, :] = left_h
    left[MEM:, :] = left_l

    def z_copy(off):
        to, device = at.along(off)
        return remote(z_out.at[to], z_got.at[at.z], z_sem, off, device)

    def memory_states(m):
        def four(i, run):
            for k in range(4):
                c = 4 * i + k
                locals_[c, m] = run.astype(BF)
                run = run * totals[pl.ds(c * MEM + m, 1), :] + incs[c, m]
            return run

        run = lax.fori_loop(0, TILES // 4, four, jnp.zeros((HD, HD), F32))
        z_out[m, 0:HD, :] = run.astype(BF)
        lines = left[pl.ds(m, 1), :], left[pl.ds(MEM + m, 1), :]
        z_out[m, HD:, :] = jnp.where(row == 0, *lines).astype(BF)

    def send_states(off):
        memory_states(at.along(off)[0])
        z_copy(off).start()
        start_pair(q_copy, 2 * off - 1)
        start_pair(q_copy, 2 * off)

    loop(1, 8, send_states)
    start_pair(q_copy, TILES - 1)
    q_copy(0, 1).start()
    memory_states(at.z)
    z_got[at.z] = z_out[at.z]

    def inside_tile(c):
        meta = tile_meta(got, c)
        oh0, oh1 = tile_masks(meta)
        run = sums[pl.ds(c * MEM, MEM), :]
        middle = 0.5 * run[:, PAIR - 1 : PAIR]
        up = jnp.exp(run - middle) * SCALE
        down_h, down_l = split_rows((oh0 + oh1) * jnp.exp(middle - run))
        below = jnp.concatenate([down_h, down_l, down_h, down_l], axis=0).astype(BF)
        vt = pair_values(got, c)
        qt = jnp.concatenate([q_got[2 * c], q_got[2 * c + 1]], axis=1)
        scores = dot(pair_keys(got, c), qt)
        reach = jnp.exp(run) * SCALE
        for j, oh in enumerate((oh0, oh1)):
            up_h, up_l = split_rows(oh * up)
            above = jnp.concatenate([up_h, up_h, up_l, up_l], axis=0).astype(BF)
            decay = lax.dot_general(
                below, above, (((0,), (0,)), ((), ())), preferred_element_type=F32
            )
            weights = jnp.where(causal, scores * decay, 0.0).astype(BF)
            across = dot(side_by_side(locals_.at[c]), chosen_queries(qt, oh))
            parts[c, j] = dot(vt, weights) + across * jnp.sum(oh * reach, axis=0, keepdims=True)

    def inside(t):
        for core in (0, 1):
            q_copy(t, core).wait_recv()
        inside_tile(at.source(t, 0)[0])

    q_copy(0, 1).wait_recv()
    inside_tile(at.source(0, 0)[0])
    loop(1, FIRST, inside)

    loop(1, 8, lambda off: z_copy(off).wait_recv())
    entering = jnp.zeros((HD, HD), F32)
    for z in range(8):
        e_out[z] = entering.astype(BF)
        left = z_got[z, HD : HD + META, :].astype(F32)
        entering = entering * (left[0:1, :] + left[1:2, :]) + z_got[z, 0:HD, :].astype(F32)

    def e_copy(off):
        to, device = at.along(off)
        return remote(e_out.at[to], e_got.at[at.z], e_sem, off, device)

    loop(1, 8, lambda off: e_copy(off).start())
    e_got[at.z] = e_out[at.z]

    loop(FIRST, TILES, inside)

    loop(1, 8, lambda off: e_copy(off).wait_recv())
    gain = gain_here[pl.ds(me, 1), :]

    def finish_tile(c):
        meta = tile_meta(got, c)
        qt = jnp.concatenate([q_got[2 * c], q_got[2 * c + 1]], axis=1)
        base = bases[pl.ds(c * MEM, MEM), :][:, 0:1]
        reach = jnp.exp(sums[pl.ds(c * MEM, MEM), :] + base) * SCALE
        mixed = jnp.zeros((HD, PAIR), F32)
        for j, oh in enumerate(tile_masks(meta)):
            across = dot(side_by_side(e_got), chosen_queries(qt, oh))
            full = parts[c, j] + across * jnp.sum(oh * reach, axis=0, keepdims=True)
            square = jnp.mean(full * full, axis=0, keepdims=True)
            weight = meta[3 + 2 * j : 4 + 2 * j, :] + meta[4 + 2 * j : 5 + 2 * j, :]
            mixed = mixed + full * (lax.rsqrt(square + 1e-06) * weight)
        return (mixed.T * gain).astype(BF)

    def o_copy(chip, core):
        _, d, device = at.target(chip, core)
        return remote(o_out.at[d], o_got.at[me], o_sem, 2 * chip + core, device)

    def finish(t):
        c = at.target(t, 0)[0]
        done = finish_tile(c)
        o_out[2 * c] = done[0:TOK]
        o_out[2 * c + 1] = done[TOK:]
        for core in (0, 1):
            o_copy(t, core).start()

    loop(1, TILES, finish)
    home = at.target(0, 0)[0]
    done = finish_tile(home)
    o_out[2 * home] = done[0:TOK]
    o_out[2 * home + 1] = done[TOK:]
    o_copy(0, 1).start()
    o_got[me] = o_out[me]

    def unpack(s):
        out_ref[pl.ds(s, TOK, stride=HEADS), :] = o_got[s].astype(F32)

    def returned(t):
        for core in (0, 1):
            o_copy(t, core).wait_recv()
            unpack(at.source(t, core)[1])

    loop(1, TILES, returned)
    o_copy(0, 1).wait_recv()
    unpack(at.source(0, 1)[1])
    unpack(me)

    for copy in (kv_copy, q_copy, o_copy):
        copy(0, 1).wait_send()
        loop(1, TILES, lambda t, copy=copy: [copy(t, core).wait_send() for core in (0, 1)])
    for copy in (z_copy, e_copy):
        loop(1, 8, lambda off, copy=copy: copy(off).wait_send())


def shards(queries, keys, values, log_decay, routes, route_weight, gain):
    sems = [pltpu.SemaphoreType.DMA((HEADS,))] * 6 + [pltpu.SemaphoreType.DMA((8,))] * 4
    out = pl.pallas_call(
        layer_kernel,
        out_shape=jax.ShapeDtypeStruct((TOK * HEADS, HD), F32),
        in_specs=[pl.BlockSpec(memory_space=pltpu.HBM)] * 7,
        out_specs=pl.BlockSpec(memory_space=pltpu.VMEM),
        scratch_shapes=[
            pltpu.VMEM((TOK, HEADS, HD), BF),
            pltpu.VMEM((TOK, HEADS, HD), BF),
            pltpu.VMEM((TOK, HEADS, HD), BF),
            pltpu.VMEM((HEADS, TOK), BF),
            pltpu.VMEM((2, TOK), jnp.int32),
            pltpu.VMEM((2, TOK), F32),
            pltpu.VMEM((HEADS, HD), F32),
            pltpu.VMEM((TOK * HEADS, HD), F32),
            pltpu.VMEM((TOK * HEADS, HD), F32),
            pltpu.VMEM((HEADS, TOK), F32),
            pltpu.VMEM((HEADS, SLAB, HD), BF),
            pltpu.VMEM((HEADS, SLAB, HD), BF),
            pltpu.VMEM((HEADS, HD, TOK), BF),
            pltpu.VMEM((HEADS, HD, TOK), BF),
            pltpu.VMEM((HEADS, TOK, HD), BF),
            pltpu.VMEM((HEADS, TOK, HD), BF),
            pltpu.VMEM((MEM, HD + META, HD), BF),
            pltpu.VMEM((MEM, HD + META, HD), BF),
            pltpu.VMEM((8, HD, HD), BF),
            pltpu.VMEM((8, HD, HD), BF),
            pltpu.VMEM((2 * MEM, HD), F32),
            pltpu.VMEM((TILES * MEM, HD), F32),
            pltpu.VMEM((TILES * MEM, PAIR), F32),
            pltpu.VMEM((TILES * MEM, HD), F32),
            pltpu.VMEM((TILES, MEM, HD, HD), F32),
            pltpu.VMEM((TILES, MEM, HD, HD), BF),
            pltpu.VMEM((TILES, 2, HD, PAIR), F32),
            *sems,
            pltpu.SemaphoreType.DMA((7,)),
        ],
        compiler_params=pltpu.CompilerParams(
            collective_id=0, has_side_effects=True, vmem_limit_bytes=60 * 1024 * 1024
        ),
        cost_estimate=pl.CostEstimate(
            flops=8 * 10**9, bytes_accessed=6 * 2**20, transcendentals=10**6
        ),
    )(
        queries[0],
        keys[0],
        values[0],
        log_decay[0].T,
        routes[0].T,
        route_weight[0].T,
        gain.reshape(HEADS, HD),
    )
    return out.astype(BF).reshape(1, TOK, HEADS, HD)


def solution(mesh):
    finer = Mesh(mesh.devices.reshape(4, 2, 8, 4), ("mem_0", "mem_1", "ctx_0", "ctx_1"))
    ctx = ("ctx_0", "ctx_1")
    mem = ("mem_0", "mem_1")
    return jax.shard_map(
        shards,
        mesh=finer,
        in_specs=(
            P(ctx, mem, None, None),
            P(ctx, mem, None, None),
            P(ctx, mem, None, None),
            P(ctx, mem, None),
            P(ctx, mem, None),
            P(ctx, mem, None),
            P(),
        ),
        out_specs=P(ctx, mem, None, None),
        check_vma=False,
    )
```

```python
import jax
import jax.numpy as jnp
from jax import lax
from jax.experimental import pallas as pl
from jax.experimental.pallas import tpu as pltpu
from jax.sharding import Mesh
from jax.sharding import PartitionSpec as P

HEADS = 32
HD = 128
TOK = 128
MEM = 8
META = 16
PAIR = 2 * TOK
TILES = HEADS // 2
EARLY = 6
FIRST = 1
SLAB = TOK + META + HD
BF = jnp.bfloat16
F32 = jnp.float32
SCALE = HD**-0.5
MESH = pl.DeviceIdType.MESH


def dot(a, b):
    return jnp.dot(a, b, preferred_element_type=F32)


ORDER = (
    ((0, 0), (1, 3), (3, 1), (2, 2), (1, 1), (3, 3), (1, 2), (3, 2))
    + ((2, 1), (2, 3), (0, 1), (1, 0), (0, 3), (3, 0), (0, 2), (2, 0))
)


def coded(values):
    whole = sum(v << (2 * i) for i, v in enumerate(values))
    return whole - (1 << 32) if whole >= 1 << 31 else whole


STEP_X, STEP_Y = coded([a for a, _ in ORDER]), coded([b for _, b in ORDER])


def offset(chip):
    if isinstance(chip, int):
        return ORDER[chip]
    turn = 2 * chip
    return tuple(jnp.bitwise_and(jnp.right_shift(jnp.int32(w), turn), 3) for w in (STEP_X, STEP_Y))


class Place:
    def __init__(self):
        self.x, self.y = lax.axis_index("ctx_1"), lax.axis_index("mem_0")
        self.c, self.z = lax.axis_index("mem_1"), lax.axis_index("ctx_0")
        self.me = (self.x * 4 + self.y) * 2 + self.c

    def target(self, chip, core):
        dx, dy = offset(chip)
        x, y, c = lax.rem(self.x + dx, 4), lax.rem(self.y + dy, 4), lax.rem(self.c + core, 2)
        return x * 4 + y, (x * 4 + y) * 2 + c, {"ctx_1": x, "mem_0": y, "mem_1": c}

    def source(self, chip, core):
        dx, dy = offset(chip)
        x, y, c = lax.rem(self.x + 4 - dx, 4), lax.rem(self.y + 4 - dy, 4), lax.rem(self.c + core, 2)
        return x * 4 + y, (x * 4 + y) * 2 + c

    def along(self, off):
        to = lax.rem(self.z + off, 8)
        return to, {"ctx_0": to}

    def back(self, off):
        return lax.rem(self.z + 8 - off, 8)


def remote(src, dst, sems, slot, device):
    return pltpu.make_async_remote_copy(
        src_ref=src,
        dst_ref=dst,
        send_sem=sems[0].at[slot],
        recv_sem=sems[1].at[slot],
        device_id=device,
        device_id_type=MESH,
    )


def loop(lo, hi, body):
    def step(i, _):
        body(i)
        return 0

    lax.fori_loop(lo, hi, step, 0)


def tile_meta(got, c):
    first = got[2 * c, TOK : TOK + META, :].astype(F32)
    second = got[2 * c + 1, TOK : TOK + META, :].astype(F32)
    return jnp.concatenate([first, second], axis=1)


def tile_masks(meta):
    ids = lax.broadcasted_iota(jnp.int32, (MEM, PAIR), 0).astype(F32)
    return jnp.where(meta[1:2, :] == ids, 1.0, 0.0), jnp.where(meta[2:3, :] == ids, 1.0, 0.0)


def pair_keys(got, c):
    return jnp.concatenate([got[2 * c, 0:TOK, :], got[2 * c + 1, 0:TOK, :]], axis=0)


def pair_values(got, c):
    return jnp.concatenate([got[2 * c, TOK + META :, :], got[2 * c + 1, TOK + META :, :]], axis=1)


def split_rows(rows):
    high = rows.astype(BF).astype(F32)
    return high, rows - high


def side_by_side(states):
    return jnp.concatenate([states[m] for m in range(MEM)], axis=1)


def chosen_queries(qt, oh):
    grouped = qt.reshape(HD // 16, 16, PAIR)
    parts = []
    for m in range(MEM):
        row = jnp.broadcast_to(oh[m : m + 1, :], (16, PAIR)).astype(BF)
        parts.append((grouped * row[None]).reshape(HD, PAIR))
    return jnp.concatenate(parts, axis=0)


def layer_kernel(
    q_ref,
    k_ref,
    v_ref,
    rate_ref,
    route_ref,
    weight_ref,
    gain_ref,
    out_ref,
    q_here,
    k_here,
    v_here,
    rate_here,
    route_here,
    weight_here,
    gain_here,
    flat_a,
    flat_b,
    rates,
    slabs,
    got,
    q_out,
    q_got,
    o_out,
    z_out,
    z_got,
    e_out,
    e_got,
    left,
    totals,
    sums,
    bases,
    incs,
    locals_,
    parts,
    kv_s,
    kv_r,
    q_s,
    q_r,
    o_s,
    o_r,
    z_s,
    z_r,
    e_s,
    e_r,
    in_s,
):
    at = Place()
    me = at.me
    kv_sem, q_sem, o_sem, z_sem, e_sem = (kv_s, kv_r), (q_s, q_r), (o_s, o_r), (z_s, z_r), (e_s, e_r)

    fetches = [
        pltpu.make_async_copy(there, here, in_s.at[i])
        for i, (there, here) in enumerate(
            (
                (k_ref, k_here),
                (v_ref, v_here),
                (rate_ref, rate_here),
                (route_ref, route_here),
                (weight_ref, weight_here),
                (gain_ref, gain_here),
                (q_ref, q_here),
            )
        )
    ]
    for fetch in fetches:
        fetch.start()
    barrier = pltpu.get_barrier_semaphore()

    def greet(device):
        pl.semaphore_signal(barrier, inc=1, device_id=device, device_id_type=MESH)

    greet(at.target(0, 1)[2])
    loop(1, TILES, lambda t: [greet(at.target(t, core)[2]) for core in (0, 1)])
    loop(1, 8, lambda off: greet(at.along(off)[1]))

    def widen(flat, here):
        def some(i):
            rows = here[pl.ds(i * 16, 16), :, :].astype(F32)
            flat[pl.ds(i * 16 * HEADS, 16 * HEADS), :] = rows.reshape(16 * HEADS, HD)

        loop(0, TOK // 16, some)

    fetches[0].wait()
    widen(flat_a, k_here)
    fetches[1].wait()
    widen(flat_b, v_here)
    for fetch in fetches[2:]:
        fetch.wait()
    rates[...] = rate_here[...].astype(F32)
    row = lax.broadcasted_iota(jnp.int32, (META, TOK), 0)
    named = route_here[...].astype(F32)
    high, low = split_rows(weight_here[...])
    common = jnp.zeros((META, TOK), F32)
    lines = (named[0:1], named[1:2], high[0:1], low[0:1], high[1:2], low[1:2])
    for i, line in enumerate(lines):
        common = jnp.where(row == i + 1, line, common)

    def by_head(flat, d):
        return flat[pl.ds(d, TOK, stride=HEADS), :]

    def pack_kv(d, dest, slot):
        dest[slot, 0:TOK, :] = by_head(flat_a, d).astype(BF)
        dest[slot, TOK : TOK + META, :] = jnp.where(row == 0, rates[pl.ds(d, 1), :], common).astype(BF)
        dest[slot, TOK + META :, :] = by_head(flat_b, d).T.astype(BF)

    def kv_copy(chip, core):
        _, d, device = at.target(chip, core)
        return remote(slabs.at[d], got.at[me], kv_sem, 2 * chip + core, device)

    def pack_pair(t):
        for core in (0, 1):
            d = at.target(t, core)[1]
            pack_kv(d, slabs, d)

    def others(t, act):
        @pl.when(t > 0)
        def _():
            act(t, 0)

        act(t, 1)

    def start_pair(copy, t):
        others(t, lambda chip, core: copy(chip, core).start())

    def last_is_home(i):
        return lax.rem(i + 1, TILES)

    loop(0, EARLY, lambda i: pack_pair(i + 1))
    pl.semaphore_wait(barrier, 38)
    loop(0, EARLY, lambda i: start_pair(kv_copy, i + 1))

    def pack_and_start(i):
        pack_pair(last_is_home(i))
        start_pair(kv_copy, last_is_home(i))

    loop(EARLY, TILES, pack_and_start)
    got[me] = slabs[me]

    widen(flat_a, q_here)

    def q_copy(chip, core):
        _, d, device = at.target(chip, core)
        return remote(q_out.at[d], q_got.at[me], q_sem, 2 * chip + core, device)

    def pack_q(d, dest):
        dest[d] = by_head(flat_a, d).T.astype(BF)

    loop(0, TILES, lambda t: [pack_q(at.target(t, core)[1], q_out) for core in (0, 1)])
    q_got[me] = q_out[me]

    first = lax.broadcasted_iota(jnp.int32, (PAIR, PAIR), 0)
    second = lax.broadcasted_iota(jnp.int32, (PAIR, PAIR), 1)
    causal = first <= second

    def gather_tile(c):
        meta = tile_meta(got, c)
        oh0, oh1 = tile_masks(meta)
        mask = oh0 + oh1
        upper = jnp.where(causal, 1.0, 0.0).astype(BF)
        run = dot((mask * meta[0:1, :]).astype(BF), upper)
        sums[pl.ds(c * MEM, MEM), :] = run
        total = run[:, PAIR - 1 : PAIR]
        totals[pl.ds(c * MEM, MEM), :] = jnp.broadcast_to(total, (MEM, HD))
        kept = mask * jnp.exp(total - run)
        wide = pair_values(got, c).astype(F32)
        scaled = jnp.concatenate(
            [(wide * kept[m : m + 1, :]).astype(BF) for m in range(MEM)], axis=0
        )
        incs[c] = dot(scaled, pair_keys(got, c)).reshape(MEM, HD, HD)

    def arrived(t):
        others(t, lambda chip, core: kv_copy(chip, core).wait_recv())
        gather_tile(at.source(t, 0)[0])

    loop(0, TILES, arrived)

    def add_total(c, base):
        at_c = pl.ds(c * MEM, MEM)
        total = totals[at_c, :]
        bases[at_c, :] = base
        totals[at_c, :] = jnp.exp(total)
        return base + total

    whole = lax.fori_loop(0, TILES, add_total, jnp.zeros((MEM, HD), F32))
    left_h, left_l = split_rows(jnp.exp(whole))
    left[0:MEM, :] = left_h
    left[MEM:, :] = left_l

    def z_copy(off):
        to, device = at.along(off)
        return remote(z_out.at[to], z_got.at[at.z], z_sem, off, device)

    def memory_states(m):
        def four(i, run):
            for k in range(4):
                c = 4 * i + k
                locals_[c, m] = run.astype(BF)
                run = run * totals[pl.ds(c * MEM + m, 1), :] + incs[c, m]
            return run

        run = lax.fori_loop(0, TILES // 4, four, jnp.zeros((HD, HD), F32))
        z_out[m, 0:HD, :] = run.astype(BF)
        lines = left[pl.ds(m, 1), :], left[pl.ds(MEM + m, 1), :]
        z_out[m, HD:, :] = jnp.where(row == 0, *lines).astype(BF)

    def send_states(off):
        memory_states(at.along(off)[0])
        z_copy(off).start()
        start_pair(q_copy, 2 * off - 1)
        start_pair(q_copy, 2 * off)

    q_copy(0, 1).start()
    loop(1, 8, send_states)
    start_pair(q_copy, TILES - 1)
    memory_states(at.z)
    z_got[at.z] = z_out[at.z]

    def inside_tile(c):
        meta = tile_meta(got, c)
        oh0, oh1 = tile_masks(meta)
        run = sums[pl.ds(c * MEM, MEM), :]
        middle = 0.5 * run[:, PAIR - 1 : PAIR]
        up = jnp.exp(run - middle) * SCALE
        down_h, down_l = split_rows((oh0 + oh1) * jnp.exp(middle - run))
        below = jnp.concatenate([down_h, down_l, down_h, down_l], axis=0).astype(BF)
        vt = pair_values(got, c)
        qt = jnp.concatenate([q_got[2 * c], q_got[2 * c + 1]], axis=1)
        scores = dot(pair_keys(got, c), qt)
        reach = jnp.exp(run) * SCALE
        for j, oh in enumerate((oh0, oh1)):
            up_h, up_l = split_rows(oh * up)
            above = jnp.concatenate([up_h, up_h, up_l, up_l], axis=0).astype(BF)
            decay = lax.dot_general(
                below, above, (((0,), (0,)), ((), ())), preferred_element_type=F32
            )
            weights = jnp.where(causal, scores * decay, 0.0).astype(BF)
            across = dot(side_by_side(locals_.at[c]), chosen_queries(qt, oh))
            parts[c, j] = dot(vt, weights) + across * jnp.sum(oh * reach, axis=0, keepdims=True)

    def e_copy(off):
        to, device = at.along(off)
        return remote(e_out.at[to], e_got.at[at.z], e_sem, off, device)

    def compose():
        loop(1, 8, lambda off: z_copy(off).wait_recv())
        entering = jnp.zeros((HD, HD), F32)
        for z in range(8):
            e_out[z] = entering.astype(BF)
            kept = z_got[z, HD : HD + META, :].astype(F32)
            entering = entering * (kept[0:1, :] + kept[1:2, :]) + z_got[z, 0:HD, :].astype(F32)
        loop(1, 8, lambda off: e_copy(off).start())
        e_got[at.z] = e_out[at.z]

    def inside(t):
        pl.when(t == FIRST)(compose)
        others(t, lambda chip, core: q_copy(chip, core).wait_recv())
        inside_tile(at.source(t, 0)[0])

    loop(0, TILES, inside)
    for copy in (kv_copy, q_copy):
        sent = lambda chip, core, copy=copy: copy(chip, core).wait_send()
        loop(0, TILES, lambda t, sent=sent: others(t, sent))
    loop(1, 8, lambda off: z_copy(off).wait_send())

    loop(1, 8, lambda off: e_copy(off).wait_recv())
    gain = gain_here[pl.ds(me, 1), :]

    def finish_tile(c):
        meta = tile_meta(got, c)
        qt = jnp.concatenate([q_got[2 * c], q_got[2 * c + 1]], axis=1)
        base = bases[pl.ds(c * MEM, MEM), :][:, 0:1]
        reach = jnp.exp(sums[pl.ds(c * MEM, MEM), :] + base) * SCALE
        mixed = jnp.zeros((HD, PAIR), F32)
        for j, oh in enumerate(tile_masks(meta)):
            across = dot(side_by_side(e_got), chosen_queries(qt, oh))
            full = parts[c, j] + across * jnp.sum(oh * reach, axis=0, keepdims=True)
            square = jnp.mean(full * full, axis=0, keepdims=True)
            weight = meta[3 + 2 * j : 4 + 2 * j, :] + meta[4 + 2 * j : 5 + 2 * j, :]
            mixed = mixed + full * (lax.rsqrt(square + 1e-06) * weight)
        return (mixed.T * gain).astype(BF)

    def o_copy(chip, core):
        _, d, device = at.target(chip, core)
        return remote(o_out.at[d], out_ref.at[me], o_sem, 0, device)

    def finish(i):
        t = last_is_home(i)
        c = at.target(t, 0)[0]
        done = finish_tile(c)
        o_out[2 * c] = done[0:TOK]
        o_out[2 * c + 1] = done[TOK:]
        start_pair(o_copy, t)

    loop(0, TILES, finish)
    own = pltpu.make_async_copy(o_out.at[me], out_ref.at[me], in_s.at[0])
    own.start()
    loop(1, 8, lambda off: e_copy(off).wait_send())
    own.wait()
    every = pl.ds(0, HEADS - 1)
    whole_out = remote(o_out.at[every], out_ref.at[every], o_sem, 0, at.target(0, 1)[2])
    whole_out.wait_recv()
    whole_out.wait_send()


def shards(queries, keys, values, log_decay, routes, route_weight, gain):
    sems = [pltpu.SemaphoreType.DMA((HEADS,))] * 4 + [pltpu.SemaphoreType.DMA((1,))] * 2 + [pltpu.SemaphoreType.DMA((8,))] * 4
    out = pl.pallas_call(
        layer_kernel,
        out_shape=jax.ShapeDtypeStruct((HEADS, TOK, HD), BF),
        in_specs=[pl.BlockSpec(memory_space=pltpu.HBM)] * 7,
        out_specs=pl.BlockSpec(memory_space=pltpu.HBM),
        scratch_shapes=[
            pltpu.VMEM((TOK, HEADS, HD), BF),
            pltpu.VMEM((TOK, HEADS, HD), BF),
            pltpu.VMEM((TOK, HEADS, HD), BF),
            pltpu.VMEM((HEADS, TOK), BF),
            pltpu.VMEM((2, TOK), jnp.int32),
            pltpu.VMEM((2, TOK), F32),
            pltpu.VMEM((HEADS, HD), F32),
            pltpu.VMEM((TOK * HEADS, HD), F32),
            pltpu.VMEM((TOK * HEADS, HD), F32),
            pltpu.VMEM((HEADS, TOK), F32),
            pltpu.VMEM((HEADS, SLAB, HD), BF),
            pltpu.VMEM((HEADS, SLAB, HD), BF),
            pltpu.VMEM((HEADS, HD, TOK), BF),
            pltpu.VMEM((HEADS, HD, TOK), BF),
            pltpu.VMEM((HEADS, TOK, HD), BF),
            pltpu.VMEM((MEM, HD + META, HD), BF),
            pltpu.VMEM((MEM, HD + META, HD), BF),
            pltpu.VMEM((8, HD, HD), BF),
            pltpu.VMEM((8, HD, HD), BF),
            pltpu.VMEM((2 * MEM, HD), F32),
            pltpu.VMEM((TILES * MEM, HD), F32),
            pltpu.VMEM((TILES * MEM, PAIR), F32),
            pltpu.VMEM((TILES * MEM, HD), F32),
            pltpu.VMEM((TILES, MEM, HD, HD), F32),
            pltpu.VMEM((TILES, MEM, HD, HD), BF),
            pltpu.VMEM((TILES, 2, HD, PAIR), F32),
            *sems,
            pltpu.SemaphoreType.DMA((7,)),
        ],
        compiler_params=pltpu.CompilerParams(
            collective_id=0, has_side_effects=True, vmem_limit_bytes=60 * 1024 * 1024
        ),
        cost_estimate=pl.CostEstimate(
            flops=8 * 10**9, bytes_accessed=6 * 2**20, transcendentals=10**6
        ),
    )(
        queries[0],
        keys[0],
        values[0],
        log_decay[0].T,
        routes[0].T,
        route_weight[0].T,
        gain.reshape(HEADS, HD),
    )
    return jnp.swapaxes(out, 0, 1)[None]


def solution(mesh):
    finer = Mesh(mesh.devices.reshape(4, 2, 8, 4), ("mem_0", "mem_1", "ctx_0", "ctx_1"))
    ctx = ("ctx_0", "ctx_1")
    mem = ("mem_0", "mem_1")
    return jax.shard_map(
        shards,
        mesh=finer,
        in_specs=(
            P(ctx, mem, None, None),
            P(ctx, mem, None, None),
            P(ctx, mem, None, None),
            P(ctx, mem, None),
            P(ctx, mem, None),
            P(ctx, mem, None),
            P(),
        ),
        out_specs=P(ctx, mem, None, None),
        check_vma=False,
    )
```

```python
import jax
import jax.numpy as jnp
from jax import lax
from jax.experimental import pallas as pl
from jax.experimental.pallas import tpu as pltpu
from jax.sharding import Mesh
from jax.sharding import PartitionSpec as P

HEADS = 32
HD = 128
TOK = 128
MEM = 8
META = 16
PAIR = 2 * TOK
TILES = HEADS // 2
EARLY = 6
SLAB = TOK + META + HD
BF = jnp.bfloat16
F32 = jnp.float32
SCALE = HD**-0.5
MESH = pl.DeviceIdType.MESH


def dot(a, b):
    return jnp.dot(a, b, preferred_element_type=F32)


ORDER = (
    ((0, 0), (1, 3), (3, 1), (2, 2), (1, 1), (3, 3), (1, 2), (3, 2))
    + ((2, 1), (2, 3), (0, 1), (1, 0), (0, 3), (3, 0), (0, 2), (2, 0))
)


def coded(values):
    whole = sum(v << (2 * i) for i, v in enumerate(values))
    return whole - (1 << 32) if whole >= 1 << 31 else whole


STEP_X, STEP_Y = coded([a for a, _ in ORDER]), coded([b for _, b in ORDER])


def offset(chip):
    if isinstance(chip, int):
        return ORDER[chip]
    turn = 2 * chip
    return tuple(jnp.bitwise_and(jnp.right_shift(jnp.int32(w), turn), 3) for w in (STEP_X, STEP_Y))


class Place:
    def __init__(self):
        self.x, self.y = lax.axis_index("ctx_1"), lax.axis_index("mem_0")
        self.c, self.z = lax.axis_index("mem_1"), lax.axis_index("ctx_0")
        self.me = (self.x * 4 + self.y) * 2 + self.c

    def target(self, chip, core):
        dx, dy = offset(chip)
        x, y, c = lax.rem(self.x + dx, 4), lax.rem(self.y + dy, 4), lax.rem(self.c + core, 2)
        return x * 4 + y, (x * 4 + y) * 2 + c, {"ctx_1": x, "mem_0": y, "mem_1": c}

    def source(self, chip, core):
        dx, dy = offset(chip)
        x, y, c = lax.rem(self.x + 4 - dx, 4), lax.rem(self.y + 4 - dy, 4), lax.rem(self.c + core, 2)
        return x * 4 + y, (x * 4 + y) * 2 + c

    def along(self, off):
        to = lax.rem(self.z + off, 8)
        return to, {"ctx_0": to}

    def back(self, off):
        return lax.rem(self.z + 8 - off, 8)


def remote(src, dst, sems, slot, device):
    return pltpu.make_async_remote_copy(
        src_ref=src,
        dst_ref=dst,
        send_sem=sems[0].at[slot],
        recv_sem=sems[1].at[slot],
        device_id=device,
        device_id_type=MESH,
    )


def loop(lo, hi, body):
    def step(i, _):
        body(i)
        return 0

    lax.fori_loop(lo, hi, step, 0)


def tile_meta(got, c):
    first = got[2 * c, TOK : TOK + META, :].astype(F32)
    second = got[2 * c + 1, TOK : TOK + META, :].astype(F32)
    return jnp.concatenate([first, second], axis=1)


def tile_masks(meta):
    ids = lax.broadcasted_iota(jnp.int32, (MEM, PAIR), 0).astype(F32)
    return jnp.where(meta[1:2, :] == ids, 1.0, 0.0), jnp.where(meta[2:3, :] == ids, 1.0, 0.0)


def pair_keys(got, c):
    return jnp.concatenate([got[2 * c, 0:TOK, :], got[2 * c + 1, 0:TOK, :]], axis=0)


def pair_values(got, c):
    return jnp.concatenate([got[2 * c, TOK + META :, :], got[2 * c + 1, TOK + META :, :]], axis=1)


def split_rows(rows):
    high = rows.astype(BF).astype(F32)
    return high, rows - high


def side_by_side(states):
    return jnp.concatenate([states[m] for m in range(MEM)], axis=1)


def chosen_queries(qt, oh):
    grouped = qt.reshape(HD // 16, 16, PAIR)
    parts = []
    for m in range(MEM):
        row = jnp.broadcast_to(oh[m : m + 1, :], (16, PAIR)).astype(BF)
        parts.append((grouped * row[None]).reshape(HD, PAIR))
    return jnp.concatenate(parts, axis=0)


def layer_kernel(
    q_ref,
    k_ref,
    v_ref,
    rate_ref,
    route_ref,
    weight_ref,
    gain_ref,
    out_ref,
    q_here,
    k_here,
    v_here,
    rate_here,
    route_here,
    weight_here,
    gain_here,
    flat_a,
    flat_b,
    rates,
    slabs,
    got,
    q_out,
    q_got,
    o_out,
    z_out,
    z_got,
    e_out,
    e_got,
    left,
    totals,
    sums,
    bases,
    incs,
    locals_,
    parts,
    decays,
    reaches,
    kv_s,
    kv_r,
    q_s,
    q_r,
    o_s,
    o_r,
    z_s,
    z_r,
    e_s,
    e_r,
    in_s,
):
    at = Place()
    me = at.me
    kv_sem, q_sem, o_sem, z_sem, e_sem = (kv_s, kv_r), (q_s, q_r), (o_s, o_r), (z_s, z_r), (e_s, e_r)

    fetches = [
        pltpu.make_async_copy(there, here, in_s.at[i])
        for i, (there, here) in enumerate(
            (
                (k_ref, k_here),
                (v_ref, v_here),
                (rate_ref, rate_here),
                (route_ref, route_here),
                (weight_ref, weight_here),
                (gain_ref, gain_here),
                (q_ref, q_here),
            )
        )
    ]
    for fetch in fetches:
        fetch.start()
    barrier = pltpu.get_barrier_semaphore()

    def greet(device):
        pl.semaphore_signal(barrier, inc=1, device_id=device, device_id_type=MESH)

    greet(at.target(0, 1)[2])
    loop(1, TILES, lambda t: [greet(at.target(t, core)[2]) for core in (0, 1)])
    loop(1, 8, lambda off: greet(at.along(off)[1]))

    def widen(flat, here):
        def some(i):
            rows = here[pl.ds(i * 16, 16), :, :].astype(F32)
            flat[pl.ds(i * 16 * HEADS, 16 * HEADS), :] = rows.reshape(16 * HEADS, HD)

        loop(0, TOK // 16, some)

    fetches[0].wait()
    widen(flat_a, k_here)
    fetches[1].wait()
    widen(flat_b, v_here)
    for fetch in fetches[2:]:
        fetch.wait()
    rates[...] = rate_here[...].astype(F32)
    row = lax.broadcasted_iota(jnp.int32, (META, TOK), 0)
    named = route_here[...].astype(F32)
    high, low = split_rows(weight_here[...])
    common = jnp.zeros((META, TOK), F32)
    lines = (named[0:1], named[1:2], high[0:1], low[0:1], high[1:2], low[1:2])
    for i, line in enumerate(lines):
        common = jnp.where(row == i + 1, line, common)

    def by_head(flat, d):
        return flat[pl.ds(d, TOK, stride=HEADS), :]

    def pack_kv(d, dest, slot):
        dest[slot, 0:TOK, :] = by_head(flat_a, d).astype(BF)
        dest[slot, TOK : TOK + META, :] = jnp.where(row == 0, rates[pl.ds(d, 1), :], common).astype(BF)
        dest[slot, TOK + META :, :] = by_head(flat_b, d).T.astype(BF)

    def kv_copy(chip, core):
        _, d, device = at.target(chip, core)
        return remote(slabs.at[d], got.at[me], kv_sem, 2 * chip + core, device)

    def pack_pair(t):
        for core in (0, 1):
            d = at.target(t, core)[1]
            pack_kv(d, slabs, d)

    def others(t, act):
        @pl.when(t > 0)
        def _():
            act(t, 0)

        act(t, 1)

    def start_pair(copy, t):
        others(t, lambda chip, core: copy(chip, core).start())

    def last_is_home(i):
        return lax.rem(i + 1, TILES)

    loop(0, EARLY, lambda i: pack_pair(i + 1))
    pl.semaphore_wait(barrier, 38)
    loop(0, EARLY, lambda i: start_pair(kv_copy, i + 1))

    def pack_and_start(i):
        pack_pair(last_is_home(i))
        start_pair(kv_copy, last_is_home(i))

    loop(EARLY, TILES, pack_and_start)
    got[me] = slabs[me]

    widen(flat_a, q_here)

    def q_copy(chip, core):
        _, d, device = at.target(chip, core)
        return remote(q_out.at[d], q_got.at[me], q_sem, 2 * chip + core, device)

    def pack_q(d, dest):
        dest[d] = by_head(flat_a, d).T.astype(BF)

    loop(0, TILES, lambda t: [pack_q(at.target(t, core)[1], q_out) for core in (0, 1)])
    q_got[me] = q_out[me]

    first = lax.broadcasted_iota(jnp.int32, (PAIR, PAIR), 0)
    second = lax.broadcasted_iota(jnp.int32, (PAIR, PAIR), 1)
    causal = first <= second

    def gather_tile(c):
        meta = tile_meta(got, c)
        oh0, oh1 = tile_masks(meta)
        mask = oh0 + oh1
        upper = jnp.where(causal, 1.0, 0.0).astype(BF)
        run = dot((mask * meta[0:1, :]).astype(BF), upper)
        sums[pl.ds(c * MEM, MEM), :] = run
        total = run[:, PAIR - 1 : PAIR]
        totals[pl.ds(c * MEM, MEM), :] = jnp.broadcast_to(total, (MEM, HD))
        kept = mask * jnp.exp(total - run)
        wide = pair_values(got, c).astype(F32)
        scaled = jnp.concatenate(
            [(wide * kept[m : m + 1, :]).astype(BF) for m in range(MEM)], axis=0
        )
        incs[c] = dot(scaled, pair_keys(got, c)).reshape(MEM, HD, HD)
        middle = 0.5 * total
        up = jnp.exp(run - middle) * SCALE
        reach = jnp.exp(run) * SCALE
        down_h, down_l = split_rows(mask * jnp.exp(middle - run))
        below = jnp.concatenate([down_h, down_l, down_h, down_l], axis=0).astype(BF)
        for j, oh in enumerate((oh0, oh1)):
            up_h, up_l = split_rows(oh * up)
            above = jnp.concatenate([up_h, up_h, up_l, up_l], axis=0).astype(BF)
            decay = lax.dot_general(
                below, above, (((0,), (0,)), ((), ())), preferred_element_type=F32
            )
            decays[c, j] = jnp.where(causal, decay, 0.0)
            reaches[c, j : j + 1, :] = jnp.sum(oh * reach, axis=0, keepdims=True)

    def arrived(t):
        others(t, lambda chip, core: kv_copy(chip, core).wait_recv())
        gather_tile(at.source(t, 0)[0])

    loop(0, TILES, arrived)

    def add_total(c, base):
        at_c = pl.ds(c * MEM, MEM)
        total = totals[at_c, :]
        bases[at_c, :] = base
        totals[at_c, :] = jnp.exp(total)
        return base + total

    whole = lax.fori_loop(0, TILES, add_total, jnp.zeros((MEM, HD), F32))
    left_h, left_l = split_rows(jnp.exp(whole))
    left[0:MEM, :] = left_h
    left[MEM:, :] = left_l

    def z_copy(off):
        to, device = at.along(off)
        return remote(z_out.at[to], z_got.at[at.z], z_sem, off, device)

    def memory_states(m):
        def four(i, run):
            for k in range(4):
                c = 4 * i + k
                locals_[c, m] = run.astype(BF)
                run = run * totals[pl.ds(c * MEM + m, 1), :] + incs[c, m]
            return run

        run = lax.fori_loop(0, TILES // 4, four, jnp.zeros((HD, HD), F32))
        z_out[m, 0:HD, :] = run.astype(BF)
        lines = left[pl.ds(m, 1), :], left[pl.ds(MEM + m, 1), :]
        z_out[m, HD:, :] = jnp.where(row == 0, *lines).astype(BF)

    def send_states(off):
        memory_states(at.along(off)[0])
        z_copy(off).start()
        start_pair(q_copy, 2 * off - 1)
        start_pair(q_copy, 2 * off)

    q_copy(0, 1).start()
    loop(1, 8, send_states)
    start_pair(q_copy, TILES - 1)
    memory_states(at.z)
    z_got[at.z] = z_out[at.z]

    def inside_tile(c):
        meta = tile_meta(got, c)
        oh0, oh1 = tile_masks(meta)
        vt = pair_values(got, c)
        qt = jnp.concatenate([q_got[2 * c], q_got[2 * c + 1]], axis=1)
        scores = dot(pair_keys(got, c), qt)
        before = side_by_side(locals_.at[c])
        for j, oh in enumerate((oh0, oh1)):
            weights = (scores * decays[c, j]).astype(BF)
            across = dot(before, chosen_queries(qt, oh))
            parts[c, j] = dot(vt, weights) + across * reaches[c, j : j + 1, :]

    def e_copy(off):
        to, device = at.along(off)
        return remote(e_out.at[to], e_got.at[at.z], e_sem, off, device)

    def compose():
        loop(1, 8, lambda off: z_copy(off).wait_recv())
        entering = jnp.zeros((HD, HD), F32)
        for z in range(8):
            e_out[z] = entering.astype(BF)
            kept = z_got[z, HD : HD + META, :].astype(F32)
            entering = entering * (kept[0:1, :] + kept[1:2, :]) + z_got[z, 0:HD, :].astype(F32)
        loop(1, 8, lambda off: e_copy(off).start())
        e_got[at.z] = e_out[at.z]

    def inside(i):
        for t in (2 * i, 2 * i + 1):
            others(t, lambda chip, core: q_copy(chip, core).wait_recv())
        for t in (2 * i, 2 * i + 1):
            inside_tile(at.source(t, 0)[0])

    compose()
    loop(0, TILES // 2, inside)
    for copy in (kv_copy, q_copy):
        sent = lambda chip, core, copy=copy: copy(chip, core).wait_send()
        loop(0, TILES, lambda t, sent=sent: others(t, sent))
    loop(1, 8, lambda off: z_copy(off).wait_send())

    loop(1, 8, lambda off: e_copy(off).wait_recv())
    gain = gain_here[pl.ds(me, 1), :]

    def finish_tile(c):
        meta = tile_meta(got, c)
        qt = jnp.concatenate([q_got[2 * c], q_got[2 * c + 1]], axis=1)
        base = bases[pl.ds(c * MEM, MEM), :][:, 0:1]
        reach = jnp.exp(sums[pl.ds(c * MEM, MEM), :] + base) * SCALE
        mixed = jnp.zeros((HD, PAIR), F32)
        for j, oh in enumerate(tile_masks(meta)):
            across = dot(side_by_side(e_got), chosen_queries(qt, oh))
            full = parts[c, j] + across * jnp.sum(oh * reach, axis=0, keepdims=True)
            square = jnp.mean(full * full, axis=0, keepdims=True)
            weight = meta[3 + 2 * j : 4 + 2 * j, :] + meta[4 + 2 * j : 5 + 2 * j, :]
            mixed = mixed + full * (lax.rsqrt(square + 1e-06) * weight)
        return (mixed.T * gain).astype(BF)

    def o_copy(chip, core):
        _, d, device = at.target(chip, core)
        return remote(o_out.at[d], out_ref.at[me], o_sem, 0, device)

    def finish(i):
        t = last_is_home(i)
        c = at.target(t, 0)[0]
        done = finish_tile(c)
        o_out[2 * c] = done[0:TOK]
        o_out[2 * c + 1] = done[TOK:]
        start_pair(o_copy, t)

    loop(0, TILES, finish)
    own = pltpu.make_async_copy(o_out.at[me], out_ref.at[me], in_s.at[0])
    own.start()
    loop(1, 8, lambda off: e_copy(off).wait_send())
    own.wait()
    every = pl.ds(0, HEADS - 1)
    whole_out = remote(o_out.at[every], out_ref.at[every], o_sem, 0, at.target(0, 1)[2])
    whole_out.wait_recv()
    whole_out.wait_send()


def shards(queries, keys, values, log_decay, routes, route_weight, gain):
    sems = [pltpu.SemaphoreType.DMA((HEADS,))] * 4 + [pltpu.SemaphoreType.DMA((1,))] * 2 + [pltpu.SemaphoreType.DMA((8,))] * 4
    out = pl.pallas_call(
        layer_kernel,
        out_shape=jax.ShapeDtypeStruct((HEADS, TOK, HD), BF),
        in_specs=[pl.BlockSpec(memory_space=pltpu.HBM)] * 7,
        out_specs=pl.BlockSpec(memory_space=pltpu.HBM),
        scratch_shapes=[
            pltpu.VMEM((TOK, HEADS, HD), BF),
            pltpu.VMEM((TOK, HEADS, HD), BF),
            pltpu.VMEM((TOK, HEADS, HD), BF),
            pltpu.VMEM((HEADS, TOK), BF),
            pltpu.VMEM((2, TOK), jnp.int32),
            pltpu.VMEM((2, TOK), F32),
            pltpu.VMEM((HEADS, HD), F32),
            pltpu.VMEM((TOK * HEADS, HD), F32),
            pltpu.VMEM((TOK * HEADS, HD), F32),
            pltpu.VMEM((HEADS, TOK), F32),
            pltpu.VMEM((HEADS, SLAB, HD), BF),
            pltpu.VMEM((HEADS, SLAB, HD), BF),
            pltpu.VMEM((HEADS, HD, TOK), BF),
            pltpu.VMEM((HEADS, HD, TOK), BF),
            pltpu.VMEM((HEADS, TOK, HD), BF),
            pltpu.VMEM((MEM, HD + META, HD), BF),
            pltpu.VMEM((MEM, HD + META, HD), BF),
            pltpu.VMEM((8, HD, HD), BF),
            pltpu.VMEM((8, HD, HD), BF),
            pltpu.VMEM((2 * MEM, HD), F32),
            pltpu.VMEM((TILES * MEM, HD), F32),
            pltpu.VMEM((TILES * MEM, PAIR), F32),
            pltpu.VMEM((TILES * MEM, HD), F32),
            pltpu.VMEM((TILES, MEM, HD, HD), F32),
            pltpu.VMEM((TILES, MEM, HD, HD), BF),
            pltpu.VMEM((TILES, 2, HD, PAIR), F32),
            pltpu.VMEM((TILES, 2, PAIR, PAIR), F32),
            pltpu.VMEM((TILES, 8, PAIR), F32),
            *sems,
            pltpu.SemaphoreType.DMA((7,)),
        ],
        compiler_params=pltpu.CompilerParams(
            collective_id=0, has_side_effects=True, vmem_limit_bytes=60 * 1024 * 1024
        ),
        cost_estimate=pl.CostEstimate(
            flops=8 * 10**9, bytes_accessed=6 * 2**20, transcendentals=10**6
        ),
    )(
        queries[0],
        keys[0],
        values[0],
        log_decay[0].T,
        routes[0].T,
        route_weight[0].T,
        gain.reshape(HEADS, HD),
    )
    return jnp.swapaxes(out, 0, 1)[None]


def solution(mesh):
    finer = Mesh(mesh.devices.reshape(4, 2, 8, 4), ("mem_0", "mem_1", "ctx_0", "ctx_1"))
    ctx = ("ctx_0", "ctx_1")
    mem = ("mem_0", "mem_1")
    return jax.shard_map(
        shards,
        mesh=finer,
        in_specs=(
            P(ctx, mem, None, None),
            P(ctx, mem, None, None),
            P(ctx, mem, None, None),
            P(ctx, mem, None),
            P(ctx, mem, None),
            P(ctx, mem, None),
            P(),
        ),
        out_specs=P(ctx, mem, None, None),
        check_vma=False,
    )
```

```python
import jax
import jax.numpy as jnp
from jax import lax
from jax.experimental import pallas as pl
from jax.experimental.pallas import tpu as pltpu
from jax.sharding import Mesh
from jax.sharding import PartitionSpec as P

HEADS = 32
HD = 128
TOK = 128
MEM = 8
META = 16
PAIR = 2 * TOK
TILES = HEADS // 2
EARLY = 6
SLAB = TOK + META + HD
BF = jnp.bfloat16
F32 = jnp.float32
SCALE = HD**-0.5
MESH = pl.DeviceIdType.MESH


def dot(a, b):
    return jnp.dot(a, b, preferred_element_type=F32)


ORDER = (
    ((0, 0), (1, 3), (3, 1), (2, 2), (1, 1), (3, 3), (1, 2), (3, 2))
    + ((2, 1), (2, 3), (0, 1), (1, 0), (0, 3), (3, 0), (0, 2), (2, 0))
)


def coded(values):
    whole = sum(v << (2 * i) for i, v in enumerate(values))
    return whole - (1 << 32) if whole >= 1 << 31 else whole


STEP_X, STEP_Y = coded([a for a, _ in ORDER]), coded([b for _, b in ORDER])


def offset(chip):
    if isinstance(chip, int):
        return ORDER[chip]
    turn = 2 * chip
    return tuple(jnp.bitwise_and(jnp.right_shift(jnp.int32(w), turn), 3) for w in (STEP_X, STEP_Y))


class Place:
    def __init__(self):
        self.x, self.y = lax.axis_index("ctx_1"), lax.axis_index("mem_0")
        self.c, self.z = lax.axis_index("mem_1"), lax.axis_index("ctx_0")
        self.me = (self.x * 4 + self.y) * 2 + self.c

    def target(self, chip, core):
        dx, dy = offset(chip)
        x, y, c = lax.rem(self.x + dx, 4), lax.rem(self.y + dy, 4), lax.rem(self.c + core, 2)
        return x * 4 + y, (x * 4 + y) * 2 + c, {"ctx_1": x, "mem_0": y, "mem_1": c}

    def source(self, chip, core):
        dx, dy = offset(chip)
        x, y, c = lax.rem(self.x + 4 - dx, 4), lax.rem(self.y + 4 - dy, 4), lax.rem(self.c + core, 2)
        return x * 4 + y, (x * 4 + y) * 2 + c

    def along(self, off):
        to = lax.rem(self.z + off, 8)
        return to, {"ctx_0": to}

    def back(self, off):
        return lax.rem(self.z + 8 - off, 8)


def remote(src, dst, sems, slot, device):
    return pltpu.make_async_remote_copy(
        src_ref=src,
        dst_ref=dst,
        send_sem=sems[0].at[slot],
        recv_sem=sems[1].at[slot],
        device_id=device,
        device_id_type=MESH,
    )


def loop(lo, hi, body):
    def step(i, _):
        body(i)
        return 0

    lax.fori_loop(lo, hi, step, 0)


def tile_meta(got, c):
    first = got[2 * c, TOK : TOK + META, :].astype(F32)
    second = got[2 * c + 1, TOK : TOK + META, :].astype(F32)
    return jnp.concatenate([first, second], axis=1)


def tile_masks(meta):
    ids = lax.broadcasted_iota(jnp.int32, (MEM, PAIR), 0).astype(F32)
    return jnp.where(meta[1:2, :] == ids, 1.0, 0.0), jnp.where(meta[2:3, :] == ids, 1.0, 0.0)


def pair_keys(got, c):
    return jnp.concatenate([got[2 * c, 0:TOK, :], got[2 * c + 1, 0:TOK, :]], axis=0)


def pair_values(got, c):
    return jnp.concatenate([got[2 * c, TOK + META :, :], got[2 * c + 1, TOK + META :, :]], axis=1)


def split_rows(rows):
    high = rows.astype(BF).astype(F32)
    return high, rows - high


def side_by_side(states):
    return jnp.concatenate([states[m] for m in range(MEM)], axis=1)


def chosen_queries(qt, oh):
    grouped = qt.reshape(HD // 16, 16, PAIR)
    parts = []
    for m in range(MEM):
        row = jnp.broadcast_to(oh[m : m + 1, :], (16, PAIR)).astype(BF)
        parts.append((grouped * row[None]).reshape(HD, PAIR))
    return jnp.concatenate(parts, axis=0)


def layer_kernel(
    q_ref,
    k_ref,
    v_ref,
    rate_ref,
    route_ref,
    weight_ref,
    gain_ref,
    out_ref,
    q_here,
    k_here,
    v_here,
    rate_here,
    route_here,
    weight_here,
    gain_here,
    flat_a,
    flat_b,
    rates,
    slabs,
    got,
    q_out,
    q_got,
    o_out,
    z_out,
    z_got,
    e_out,
    e_got,
    left,
    totals,
    sums,
    bases,
    incs,
    locals_,
    parts,
    decays,
    reaches,
    kv_s,
    kv_r,
    q_s,
    q_r,
    o_s,
    o_r,
    z_s,
    z_r,
    e_s,
    e_r,
    in_s,
):
    at = Place()
    me = at.me
    kv_sem, q_sem, o_sem, z_sem, e_sem = (kv_s, kv_r), (q_s, q_r), (o_s, o_r), (z_s, z_r), (e_s, e_r)

    fetches = [
        pltpu.make_async_copy(there, here, in_s.at[i])
        for i, (there, here) in enumerate(
            (
                (k_ref, k_here),
                (v_ref, v_here),
                (rate_ref, rate_here),
                (route_ref, route_here),
                (weight_ref, weight_here),
                (gain_ref, gain_here),
                (q_ref, q_here),
            )
        )
    ]
    for fetch in fetches:
        fetch.start()
    barrier = pltpu.get_barrier_semaphore()

    def greet(device):
        pl.semaphore_signal(barrier, inc=1, device_id=device, device_id_type=MESH)

    greet(at.target(0, 1)[2])
    loop(1, TILES, lambda t: [greet(at.target(t, core)[2]) for core in (0, 1)])
    loop(1, 8, lambda off: greet(at.along(off)[1]))

    def widen(flat, here):
        def some(i):
            rows = here[pl.ds(i * 16, 16), :, :].astype(F32)
            flat[pl.ds(i * 16 * HEADS, 16 * HEADS), :] = rows.reshape(16 * HEADS, HD)

        loop(0, TOK // 16, some)

    fetches[0].wait()
    widen(flat_a, k_here)
    fetches[1].wait()
    widen(flat_b, v_here)
    for fetch in fetches[2:]:
        fetch.wait()
    rates[...] = rate_here[...].astype(F32)
    row = lax.broadcasted_iota(jnp.int32, (META, TOK), 0)
    named = route_here[...].astype(F32)
    high, low = split_rows(weight_here[...])
    common = jnp.zeros((META, TOK), F32)
    lines = (named[0:1], named[1:2], high[0:1], low[0:1], high[1:2], low[1:2])
    for i, line in enumerate(lines):
        common = jnp.where(row == i + 1, line, common)

    def by_head(flat, d):
        return flat[pl.ds(d, TOK, stride=HEADS), :]

    def pack_kv(d, dest, slot):
        dest[slot, 0:TOK, :] = by_head(flat_a, d).astype(BF)
        dest[slot, TOK : TOK + META, :] = jnp.where(row == 0, rates[pl.ds(d, 1), :], common).astype(BF)
        dest[slot, TOK + META :, :] = by_head(flat_b, d).T.astype(BF)

    def kv_copy(chip, core):
        _, d, device = at.target(chip, core)
        return remote(slabs.at[d], got.at[me], kv_sem, 2 * chip + core, device)

    def pack_pair(t):
        for core in (0, 1):
            d = at.target(t, core)[1]
            pack_kv(d, slabs, d)

    def others(t, act):
        @pl.when(t > 0)
        def _():
            act(t, 0)

        act(t, 1)

    def start_pair(copy, t):
        others(t, lambda chip, core: copy(chip, core).start())

    def last_is_home(i):
        return lax.rem(i + 1, TILES)

    loop(0, EARLY, lambda i: pack_pair(i + 1))
    pl.semaphore_wait(barrier, 38)
    loop(0, EARLY, lambda i: start_pair(kv_copy, i + 1))

    def pack_and_start(i):
        pack_pair(last_is_home(i))
        start_pair(kv_copy, last_is_home(i))

    loop(EARLY, TILES, pack_and_start)
    got[me] = slabs[me]

    widen(flat_a, q_here)

    def q_copy(chip, core):
        _, d, device = at.target(chip, core)
        return remote(q_out.at[d], q_got.at[me], q_sem, 2 * chip + core, device)

    def pack_q(d, dest):
        dest[d] = by_head(flat_a, d).T.astype(BF)

    loop(0, TILES, lambda t: [pack_q(at.target(t, core)[1], q_out) for core in (0, 1)])
    q_got[me] = q_out[me]

    first = lax.broadcasted_iota(jnp.int32, (PAIR, PAIR), 0)
    second = lax.broadcasted_iota(jnp.int32, (PAIR, PAIR), 1)
    causal = first <= second

    def gather_tile(c):
        meta = tile_meta(got, c)
        oh0, oh1 = tile_masks(meta)
        mask = oh0 + oh1
        upper = jnp.where(causal, 1.0, 0.0).astype(BF)
        run = dot((mask * meta[0:1, :]).astype(BF), upper)
        sums[pl.ds(c * MEM, MEM), :] = run
        total = run[:, PAIR - 1 : PAIR]
        totals[pl.ds(c * MEM, MEM), :] = jnp.broadcast_to(total, (MEM, HD))
        kept = mask * jnp.exp(total - run)
        wide = pair_values(got, c).astype(F32)
        scaled = jnp.concatenate(
            [(wide * kept[m : m + 1, :]).astype(BF) for m in range(MEM)], axis=0
        )
        incs[c] = dot(scaled, pair_keys(got, c)).reshape(MEM, HD, HD)
        middle = 0.5 * total
        up = jnp.exp(run - middle) * SCALE
        reach = jnp.exp(run) * SCALE
        down_h, down_l = split_rows(mask * jnp.exp(middle - run))
        below = jnp.concatenate([down_h, down_l, down_h, down_l], axis=0).astype(BF)
        for j, oh in enumerate((oh0, oh1)):
            up_h, up_l = split_rows(oh * up)
            above = jnp.concatenate([up_h, up_h, up_l, up_l], axis=0).astype(BF)
            decay = lax.dot_general(
                below, above, (((0,), (0,)), ((), ())), preferred_element_type=F32
            )
            decays[c, j] = jnp.where(causal, decay, 0.0)
            reaches[c, j : j + 1, :] = jnp.sum(oh * reach, axis=0, keepdims=True)

    def arrived(t):
        others(t, lambda chip, core: kv_copy(chip, core).wait_recv())
        gather_tile(at.source(t, 0)[0])

    loop(0, TILES, arrived)

    whole = jnp.zeros((MEM, HD), F32)
    for c in range(TILES):
        lines = slice(c * MEM, (c + 1) * MEM)
        bases[lines, :] = whole
        total = totals[lines, :]
        totals[lines, :] = jnp.exp(total)
        whole = whole + total
    left_h, left_l = split_rows(jnp.exp(whole))
    left[0:MEM, :] = left_h
    left[MEM:, :] = left_l

    halves = (pl.ds(0, META + HD // 2), pl.ds(META + HD // 2, HD // 2))
    e_halves = (pl.ds(0, HD // 2), pl.ds(HD // 2, HD // 2))

    def z_copy(off, half):
        to, device = at.along(off)
        rows = halves[half]
        return remote(z_out.at[to, rows], z_got.at[at.z, rows], z_sem, 2 * off + half, device)

    def memory_states(m):
        def four(i, run):
            for k in range(4):
                c = 4 * i + k
                locals_[c, m] = run.astype(BF)
                run = run * totals[pl.ds(c * MEM + m, 1), :] + incs[c, m]
            return run

        run = lax.fori_loop(0, TILES // 4, four, jnp.zeros((HD, HD), F32))
        z_out[m, META:, :] = run.astype(BF)
        lines = left[pl.ds(m, 1), :], left[pl.ds(MEM + m, 1), :]
        z_out[m, 0:META, :] = jnp.where(row == 0, *lines).astype(BF)

    def send_states(off):
        memory_states(at.along(off)[0])
        z_copy(off, 0).start()
        start_pair(q_copy, 2 * off - 1)
        start_pair(q_copy, 2 * off)

    q_copy(0, 1).start()
    loop(1, 8, send_states)
    loop(1, 8, lambda off: z_copy(off, 1).start())
    start_pair(q_copy, TILES - 1)
    memory_states(at.z)
    z_got[at.z] = z_out[at.z]

    def inside_tile(c):
        meta = tile_meta(got, c)
        oh0, oh1 = tile_masks(meta)
        vt = pair_values(got, c)
        qt = jnp.concatenate([q_got[2 * c], q_got[2 * c + 1]], axis=1)
        scores = dot(pair_keys(got, c), qt)
        before = side_by_side(locals_.at[c])
        for j, oh in enumerate((oh0, oh1)):
            weights = (scores * decays[c, j]).astype(BF)
            across = dot(before, chosen_queries(qt, oh))
            parts[c, j] = dot(vt, weights) + across * reaches[c, j : j + 1, :]

    def e_copy(off, half):
        to, device = at.along(off)
        rows = e_halves[half]
        return remote(e_out.at[to, rows], e_got.at[at.z, rows], e_sem, 2 * off + half, device)

    def compose(half):
        loop(1, 8, lambda off: z_copy(off, half).wait_recv())
        entering = jnp.zeros((HD // 2, HD), F32)
        low = half * (HD // 2)
        rows = slice(low, low + HD // 2)
        given = slice(META + low, META + low + HD // 2)
        for z in range(8):
            e_out[z, rows, :] = entering.astype(BF)
            kept = z_got[z, 0:META, :].astype(F32)
            entering = entering * (kept[0:1, :] + kept[1:2, :]) + z_got[z, given, :].astype(F32)
        loop(1, 8, lambda off: e_copy(off, half).start())

    def inside(i):
        for t in (2 * i, 2 * i + 1):
            others(t, lambda chip, core: q_copy(chip, core).wait_recv())
        for t in (2 * i, 2 * i + 1):
            inside_tile(at.source(t, 0)[0])

    compose(0)
    compose(1)
    e_got[at.z] = e_out[at.z]
    loop(0, TILES // 2, inside)
    for copy in (kv_copy, q_copy):
        sent = lambda chip, core, copy=copy: copy(chip, core).wait_send()
        loop(0, TILES, lambda t, sent=sent: others(t, sent))
    loop(1, 8, lambda off: [z_copy(off, half).wait_send() for half in (0, 1)])

    loop(1, 8, lambda off: [e_copy(off, half).wait_recv() for half in (0, 1)])
    gain = gain_here[pl.ds(me, 1), :]

    def finish_tile(c):
        meta = tile_meta(got, c)
        qt = jnp.concatenate([q_got[2 * c], q_got[2 * c + 1]], axis=1)
        base = bases[pl.ds(c * MEM, MEM), :][:, 0:1]
        reach = jnp.exp(sums[pl.ds(c * MEM, MEM), :] + base) * SCALE
        mixed = jnp.zeros((HD, PAIR), F32)
        for j, oh in enumerate(tile_masks(meta)):
            across = dot(side_by_side(e_got), chosen_queries(qt, oh))
            full = parts[c, j] + across * jnp.sum(oh * reach, axis=0, keepdims=True)
            square = jnp.mean(full * full, axis=0, keepdims=True)
            weight = meta[3 + 2 * j : 4 + 2 * j, :] + meta[4 + 2 * j : 5 + 2 * j, :]
            mixed = mixed + full * (lax.rsqrt(square + 1e-06) * weight)
        return (mixed.T * gain).astype(BF)

    def o_copy(chip, core):
        _, d, device = at.target(chip, core)
        return remote(o_out.at[d], out_ref.at[me], o_sem, 0, device)

    def finish(i):
        t = last_is_home(i)
        c = at.target(t, 0)[0]
        done = finish_tile(c)
        o_out[2 * c] = done[0:TOK]
        o_out[2 * c + 1] = done[TOK:]
        start_pair(o_copy, t)

    loop(0, TILES, finish)
    own = pltpu.make_async_copy(o_out.at[me], out_ref.at[me], in_s.at[0])
    own.start()
    loop(1, 8, lambda off: [e_copy(off, half).wait_send() for half in (0, 1)])
    own.wait()
    every = pl.ds(0, HEADS - 1)
    whole_out = remote(o_out.at[every], out_ref.at[every], o_sem, 0, at.target(0, 1)[2])
    whole_out.wait_recv()
    whole_out.wait_send()


def shards(queries, keys, values, log_decay, routes, route_weight, gain):
    sems = [pltpu.SemaphoreType.DMA((HEADS,))] * 4 + [pltpu.SemaphoreType.DMA((1,))] * 2 + [pltpu.SemaphoreType.DMA((16,))] * 4
    out = pl.pallas_call(
        layer_kernel,
        out_shape=jax.ShapeDtypeStruct((HEADS, TOK, HD), BF),
        in_specs=[pl.BlockSpec(memory_space=pltpu.HBM)] * 7,
        out_specs=pl.BlockSpec(memory_space=pltpu.HBM),
        scratch_shapes=[
            pltpu.VMEM((TOK, HEADS, HD), BF),
            pltpu.VMEM((TOK, HEADS, HD), BF),
            pltpu.VMEM((TOK, HEADS, HD), BF),
            pltpu.VMEM((HEADS, TOK), BF),
            pltpu.VMEM((2, TOK), jnp.int32),
            pltpu.VMEM((2, TOK), F32),
            pltpu.VMEM((HEADS, HD), F32),
            pltpu.VMEM((TOK * HEADS, HD), F32),
            pltpu.VMEM((TOK * HEADS, HD), F32),
            pltpu.VMEM((HEADS, TOK), F32),
            pltpu.VMEM((HEADS, SLAB, HD), BF),
            pltpu.VMEM((HEADS, SLAB, HD), BF),
            pltpu.VMEM((HEADS, HD, TOK), BF),
            pltpu.VMEM((HEADS, HD, TOK), BF),
            pltpu.VMEM((HEADS, TOK, HD), BF),
            pltpu.VMEM((MEM, HD + META, HD), BF),
            pltpu.VMEM((MEM, HD + META, HD), BF),
            pltpu.VMEM((8, HD, HD), BF),
            pltpu.VMEM((8, HD, HD), BF),
            pltpu.VMEM((2 * MEM, HD), F32),
            pltpu.VMEM((TILES * MEM, HD), F32),
            pltpu.VMEM((TILES * MEM, PAIR), F32),
            pltpu.VMEM((TILES * MEM, HD), F32),
            pltpu.VMEM((TILES, MEM, HD, HD), F32),
            pltpu.VMEM((TILES, MEM, HD, HD), BF),
            pltpu.VMEM((TILES, 2, HD, PAIR), F32),
            pltpu.VMEM((TILES, 2, PAIR, PAIR), F32),
            pltpu.VMEM((TILES, 8, PAIR), F32),
            *sems,
            pltpu.SemaphoreType.DMA((7,)),
        ],
        compiler_params=pltpu.CompilerParams(
            collective_id=0, has_side_effects=True, vmem_limit_bytes=60 * 1024 * 1024
        ),
        cost_estimate=pl.CostEstimate(
            flops=8 * 10**9, bytes_accessed=6 * 2**20, transcendentals=10**6
        ),
    )(
        queries[0],
        keys[0],
        values[0],
        log_decay[0].T,
        routes[0].T,
        route_weight[0].T,
        gain.reshape(HEADS, HD),
    )
    return jnp.swapaxes(out, 0, 1)[None]


def solution(mesh):
    finer = Mesh(mesh.devices.reshape(4, 2, 8, 4), ("mem_0", "mem_1", "ctx_0", "ctx_1"))
    ctx = ("ctx_0", "ctx_1")
    mem = ("mem_0", "mem_1")
    return jax.shard_map(
        shards,
        mesh=finer,
        in_specs=(
            P(ctx, mem, None, None),
            P(ctx, mem, None, None),
            P(ctx, mem, None, None),
            P(ctx, mem, None),
            P(ctx, mem, None),
            P(ctx, mem, None),
            P(),
        ),
        out_specs=P(ctx, mem, None, None),
        check_vma=False,
    )
```

```python
import jax
import jax.numpy as jnp
from jax import lax
from jax.experimental import pallas as pl
from jax.experimental.pallas import tpu as pltpu
from jax.sharding import Mesh
from jax.sharding import PartitionSpec as P

HEADS = 32
HD = 128
TOK = 128
MEM = 8
META = 16
PAIR = 2 * TOK
TILES = HEADS // 2
EARLY = 6
ENOUGH = 12
SLAB = TOK + META + HD
BF = jnp.bfloat16
F32 = jnp.float32
SCALE = HD**-0.5
MESH = pl.DeviceIdType.MESH


def dot(a, b):
    return jnp.dot(a, b, preferred_element_type=F32)


ORDER = (
    ((0, 0), (1, 3), (3, 1), (2, 2), (1, 1), (3, 3), (1, 2), (3, 2))
    + ((2, 1), (2, 3), (0, 1), (1, 0), (0, 3), (3, 0), (0, 2), (2, 0))
)


def coded(values):
    whole = sum(v << (2 * i) for i, v in enumerate(values))
    return whole - (1 << 32) if whole >= 1 << 31 else whole


STEP_X, STEP_Y = coded([a for a, _ in ORDER]), coded([b for _, b in ORDER])


def offset(chip):
    if isinstance(chip, int):
        return ORDER[chip]
    turn = 2 * chip
    return tuple(jnp.bitwise_and(jnp.right_shift(jnp.int32(w), turn), 3) for w in (STEP_X, STEP_Y))


class Place:
    def __init__(self):
        self.x, self.y = lax.axis_index("ctx_1"), lax.axis_index("mem_0")
        self.c, self.z = lax.axis_index("mem_1"), lax.axis_index("ctx_0")
        self.me = (self.x * 4 + self.y) * 2 + self.c

    def target(self, chip, core):
        dx, dy = offset(chip)
        x, y, c = lax.rem(self.x + dx, 4), lax.rem(self.y + dy, 4), lax.rem(self.c + core, 2)
        return x * 4 + y, (x * 4 + y) * 2 + c, {"ctx_1": x, "mem_0": y, "mem_1": c}

    def source(self, chip, core):
        dx, dy = offset(chip)
        x, y, c = lax.rem(self.x + 4 - dx, 4), lax.rem(self.y + 4 - dy, 4), lax.rem(self.c + core, 2)
        return x * 4 + y, (x * 4 + y) * 2 + c

    def along(self, off):
        to = lax.rem(self.z + off, 8)
        return to, {"ctx_0": to}

    def back(self, off):
        return lax.rem(self.z + 8 - off, 8)


def remote(src, dst, sems, slot, device):
    return pltpu.make_async_remote_copy(
        src_ref=src,
        dst_ref=dst,
        send_sem=sems[0].at[slot],
        recv_sem=sems[1].at[slot],
        device_id=device,
        device_id_type=MESH,
    )


def loop(lo, hi, body):
    def step(i, _):
        body(i)
        return 0

    lax.fori_loop(lo, hi, step, 0)


def tile_meta(got, c):
    first = got[2 * c, TOK : TOK + META, :].astype(F32)
    second = got[2 * c + 1, TOK : TOK + META, :].astype(F32)
    return jnp.concatenate([first, second], axis=1)


def tile_masks(meta):
    ids = lax.broadcasted_iota(jnp.int32, (MEM, PAIR), 0).astype(F32)
    return jnp.where(meta[1:2, :] == ids, 1.0, 0.0), jnp.where(meta[2:3, :] == ids, 1.0, 0.0)


def pair_keys(got, c):
    return jnp.concatenate([got[2 * c, 0:TOK, :], got[2 * c + 1, 0:TOK, :]], axis=0)


def pair_values(got, c):
    return jnp.concatenate([got[2 * c, TOK + META :, :], got[2 * c + 1, TOK + META :, :]], axis=1)


def split_rows(rows):
    high = rows.astype(BF).astype(F32)
    return high, rows - high


def side_by_side(states):
    return jnp.concatenate([states[m] for m in range(MEM)], axis=1)


def chosen_queries(qt, oh):
    grouped = qt.reshape(HD // 16, 16, PAIR)
    parts = []
    for m in range(MEM):
        row = jnp.broadcast_to(oh[m : m + 1, :], (16, PAIR)).astype(BF)
        parts.append((grouped * row[None]).reshape(HD, PAIR))
    return jnp.concatenate(parts, axis=0)


def layer_kernel(
    q_ref,
    k_ref,
    v_ref,
    rate_ref,
    route_ref,
    weight_ref,
    gain_ref,
    out_ref,
    q_here,
    k_here,
    v_here,
    rate_here,
    route_here,
    weight_here,
    gain_here,
    flat_a,
    flat_b,
    rates,
    slabs,
    got,
    q_out,
    q_got,
    o_out,
    z_out,
    z_got,
    e_out,
    e_got,
    left,
    totals,
    sums,
    bases,
    incs,
    locals_,
    parts,
    decays,
    reaches,
    kv_s,
    kv_r,
    q_s,
    q_r,
    o_s,
    o_r,
    z_s,
    z_r,
    e_s,
    e_r,
    in_s,
):
    at = Place()
    me = at.me
    kv_sem, q_sem, o_sem, z_sem, e_sem = (kv_s, kv_r), (q_s, q_r), (o_s, o_r), (z_s, z_r), (e_s, e_r)

    fetches = [
        pltpu.make_async_copy(there, here, in_s.at[i])
        for i, (there, here) in enumerate(
            (
                (k_ref, k_here),
                (v_ref, v_here),
                (rate_ref, rate_here),
                (route_ref, route_here),
                (weight_ref, weight_here),
                (gain_ref, gain_here),
                (q_ref, q_here),
            )
        )
    ]
    for fetch in fetches:
        fetch.start()
    barrier = pltpu.get_barrier_semaphore()

    def greet(device):
        pl.semaphore_signal(barrier, inc=1, device_id=device, device_id_type=MESH)

    greet(at.target(0, 1)[2])
    loop(1, TILES, lambda t: [greet(at.target(t, core)[2]) for core in (0, 1)])
    loop(1, 8, lambda off: greet(at.along(off)[1]))

    def widen(flat, here):
        def some(i):
            rows = here[pl.ds(i * 16, 16), :, :].astype(F32)
            flat[pl.ds(i * 16 * HEADS, 16 * HEADS), :] = rows.reshape(16 * HEADS, HD)

        loop(0, TOK // 16, some)

    fetches[0].wait()
    widen(flat_a, k_here)
    fetches[1].wait()
    widen(flat_b, v_here)
    for fetch in fetches[2:]:
        fetch.wait()
    rates[...] = rate_here[...].astype(F32)
    row = lax.broadcasted_iota(jnp.int32, (META, TOK), 0)
    named = route_here[...].astype(F32)
    high, low = split_rows(weight_here[...])
    common = jnp.zeros((META, TOK), F32)
    lines = (named[0:1], named[1:2], high[0:1], low[0:1], high[1:2], low[1:2])
    for i, line in enumerate(lines):
        common = jnp.where(row == i + 1, line, common)

    def by_head(flat, d):
        return flat[pl.ds(d, TOK, stride=HEADS), :]

    def pack_kv(d, dest, slot):
        dest[slot, 0:TOK, :] = by_head(flat_a, d).astype(BF)
        dest[slot, TOK : TOK + META, :] = jnp.where(row == 0, rates[pl.ds(d, 1), :], common).astype(BF)
        dest[slot, TOK + META :, :] = by_head(flat_b, d).T.astype(BF)

    def kv_copy(chip, core):
        _, d, device = at.target(chip, core)
        return remote(slabs.at[d], got.at[me], kv_sem, 2 * chip + core, device)

    def pack_pair(t):
        for core in (0, 1):
            d = at.target(t, core)[1]
            pack_kv(d, slabs, d)

    def others(t, act):
        @pl.when(t > 0)
        def _():
            act(t, 0)

        act(t, 1)

    def start_pair(copy, t):
        others(t, lambda chip, core: copy(chip, core).start())

    def last_is_home(i):
        return lax.rem(i + 1, TILES)

    loop(0, EARLY, lambda i: pack_pair(i + 1))
    pl.semaphore_wait(barrier, 38)
    loop(0, EARLY, lambda i: start_pair(kv_copy, i + 1))

    def pack_and_start(i):
        pack_pair(last_is_home(i))
        start_pair(kv_copy, last_is_home(i))

    loop(EARLY, TILES, pack_and_start)
    got[me] = slabs[me]

    widen(flat_a, q_here)

    def q_copy(chip, core):
        _, d, device = at.target(chip, core)
        return remote(q_out.at[d], q_got.at[me], q_sem, 2 * chip + core, device)

    def pack_q(d, dest):
        dest[d] = by_head(flat_a, d).T.astype(BF)

    loop(0, TILES, lambda t: [pack_q(at.target(t, core)[1], q_out) for core in (0, 1)])
    q_got[me] = q_out[me]

    first = lax.broadcasted_iota(jnp.int32, (PAIR, PAIR), 0)
    second = lax.broadcasted_iota(jnp.int32, (PAIR, PAIR), 1)
    causal = first <= second

    def gather_tile(c):
        meta = tile_meta(got, c)
        oh0, oh1 = tile_masks(meta)
        mask = oh0 + oh1
        upper = jnp.where(causal, 1.0, 0.0).astype(BF)
        run = dot((mask * meta[0:1, :]).astype(BF), upper)
        sums[pl.ds(c * MEM, MEM), :] = run
        total = run[:, PAIR - 1 : PAIR]
        totals[pl.ds(c * MEM, MEM), :] = jnp.broadcast_to(total, (MEM, HD))
        kept = mask * jnp.exp(total - run)
        wide = pair_values(got, c).astype(F32)
        scaled = jnp.concatenate(
            [(wide * kept[m : m + 1, :]).astype(BF) for m in range(MEM)], axis=0
        )
        incs[c] = dot(scaled, pair_keys(got, c)).reshape(MEM, HD, HD)
        middle = 0.5 * total
        up = jnp.exp(run - middle) * SCALE
        reach = jnp.exp(run) * SCALE
        down_h, down_l = split_rows(mask * jnp.exp(middle - run))
        below = jnp.concatenate([down_h, down_l, down_h, down_l], axis=0).astype(BF)
        for j, oh in enumerate((oh0, oh1)):
            up_h, up_l = split_rows(oh * up)
            above = jnp.concatenate([up_h, up_h, up_l, up_l], axis=0).astype(BF)
            decay = lax.dot_general(
                below, above, (((0,), (0,)), ((), ())), preferred_element_type=F32
            )
            decays[c, j] = jnp.where(causal, decay, 0.0)
            reaches[c, j : j + 1, :] = jnp.sum(oh * reach, axis=0, keepdims=True)

    def arrived(t):
        others(t, lambda chip, core: kv_copy(chip, core).wait_recv())

        @pl.when(t == ENOUGH)
        def _():
            loop(0, TILES, lambda chip: start_pair(q_copy, chip))

        gather_tile(at.source(t, 0)[0])

    loop(0, TILES, arrived)

    whole = jnp.zeros((MEM, HD), F32)
    for c in range(TILES):
        lines = slice(c * MEM, (c + 1) * MEM)
        bases[lines, :] = whole
        total = totals[lines, :]
        totals[lines, :] = jnp.exp(total)
        whole = whole + total
    left_h, left_l = split_rows(jnp.exp(whole))
    left[0:MEM, :] = left_h
    left[MEM:, :] = left_l

    halves = (pl.ds(0, META + HD // 2), pl.ds(META + HD // 2, HD // 2))
    e_halves = (pl.ds(0, HD // 2), pl.ds(HD // 2, HD // 2))

    def z_copy(off, half):
        to, device = at.along(off)
        rows = halves[half]
        return remote(z_out.at[to, rows], z_got.at[at.z, rows], z_sem, 2 * off + half, device)

    def memory_states(m):
        def four(i, run):
            for k in range(4):
                c = 4 * i + k
                locals_[c, m] = run.astype(BF)
                run = run * totals[pl.ds(c * MEM + m, 1), :] + incs[c, m]
            return run

        run = lax.fori_loop(0, TILES // 4, four, jnp.zeros((HD, HD), F32))
        z_out[m, META:, :] = run.astype(BF)
        lines = left[pl.ds(m, 1), :], left[pl.ds(MEM + m, 1), :]
        z_out[m, 0:META, :] = jnp.where(row == 0, *lines).astype(BF)

    def send_states(off):
        memory_states(at.along(off)[0])
        z_copy(off, 0).start()

    loop(1, 8, send_states)
    loop(1, 8, lambda off: z_copy(off, 1).start())
    memory_states(at.z)
    z_got[at.z] = z_out[at.z]

    def inside_tile(c):
        meta = tile_meta(got, c)
        oh0, oh1 = tile_masks(meta)
        vt = pair_values(got, c)
        qt = jnp.concatenate([q_got[2 * c], q_got[2 * c + 1]], axis=1)
        scores = dot(pair_keys(got, c), qt)
        before = side_by_side(locals_.at[c])
        for j, oh in enumerate((oh0, oh1)):
            weights = (scores * decays[c, j]).astype(BF)
            across = dot(before, chosen_queries(qt, oh))
            parts[c, j] = dot(vt, weights) + across * reaches[c, j : j + 1, :]

    def e_copy(off, half):
        to, device = at.along(off)
        rows = e_halves[half]
        return remote(e_out.at[to, rows], e_got.at[at.z, rows], e_sem, 2 * off + half, device)

    def compose(half):
        loop(1, 8, lambda off: z_copy(off, half).wait_recv())
        entering = jnp.zeros((HD // 2, HD), F32)
        low = half * (HD // 2)
        rows = slice(low, low + HD // 2)
        given = slice(META + low, META + low + HD // 2)
        for z in range(8):
            e_out[z, rows, :] = entering.astype(BF)
            kept = z_got[z, 0:META, :].astype(F32)
            entering = entering * (kept[0:1, :] + kept[1:2, :]) + z_got[z, given, :].astype(F32)
        loop(1, 8, lambda off: e_copy(off, half).start())

    def inside(i):
        for t in (2 * i, 2 * i + 1):
            others(t, lambda chip, core: q_copy(chip, core).wait_recv())
        for t in (2 * i, 2 * i + 1):
            inside_tile(at.source(t, 0)[0])

    compose(0)
    compose(1)
    e_got[at.z] = e_out[at.z]
    loop(0, TILES // 2, inside)
    for copy in (kv_copy, q_copy):
        sent = lambda chip, core, copy=copy: copy(chip, core).wait_send()
        loop(0, TILES, lambda t, sent=sent: others(t, sent))
    loop(1, 8, lambda off: [z_copy(off, half).wait_send() for half in (0, 1)])

    loop(1, 8, lambda off: [e_copy(off, half).wait_recv() for half in (0, 1)])
    gain = gain_here[pl.ds(me, 1), :]

    def finish_tile(c):
        meta = tile_meta(got, c)
        qt = jnp.concatenate([q_got[2 * c], q_got[2 * c + 1]], axis=1)
        base = bases[pl.ds(c * MEM, MEM), :][:, 0:1]
        reach = jnp.exp(sums[pl.ds(c * MEM, MEM), :] + base) * SCALE
        mixed = jnp.zeros((HD, PAIR), F32)
        for j, oh in enumerate(tile_masks(meta)):
            across = dot(side_by_side(e_got), chosen_queries(qt, oh))
            full = parts[c, j] + across * jnp.sum(oh * reach, axis=0, keepdims=True)
            square = jnp.mean(full * full, axis=0, keepdims=True)
            weight = meta[3 + 2 * j : 4 + 2 * j, :] + meta[4 + 2 * j : 5 + 2 * j, :]
            mixed = mixed + full * (lax.rsqrt(square + 1e-06) * weight)
        return (mixed.T * gain).astype(BF)

    def o_copy(chip, core):
        _, d, device = at.target(chip, core)
        return remote(o_out.at[d], out_ref.at[me], o_sem, 0, device)

    def finish(i):
        t = last_is_home(i)
        c = at.target(t, 0)[0]
        done = finish_tile(c)
        o_out[2 * c] = done[0:TOK]
        o_out[2 * c + 1] = done[TOK:]
        start_pair(o_copy, t)

    loop(0, TILES, finish)
    own = pltpu.make_async_copy(o_out.at[me], out_ref.at[me], in_s.at[0])
    own.start()
    loop(1, 8, lambda off: [e_copy(off, half).wait_send() for half in (0, 1)])
    own.wait()
    every = pl.ds(0, HEADS - 1)
    whole_out = remote(o_out.at[every], out_ref.at[every], o_sem, 0, at.target(0, 1)[2])
    whole_out.wait_recv()
    whole_out.wait_send()


def shards(queries, keys, values, log_decay, routes, route_weight, gain):
    sems = [pltpu.SemaphoreType.DMA((HEADS,))] * 4 + [pltpu.SemaphoreType.DMA((1,))] * 2 + [pltpu.SemaphoreType.DMA((16,))] * 4
    out = pl.pallas_call(
        layer_kernel,
        out_shape=jax.ShapeDtypeStruct((HEADS, TOK, HD), BF),
        in_specs=[pl.BlockSpec(memory_space=pltpu.HBM)] * 7,
        out_specs=pl.BlockSpec(memory_space=pltpu.HBM),
        scratch_shapes=[
            pltpu.VMEM((TOK, HEADS, HD), BF),
            pltpu.VMEM((TOK, HEADS, HD), BF),
            pltpu.VMEM((TOK, HEADS, HD), BF),
            pltpu.VMEM((HEADS, TOK), BF),
            pltpu.VMEM((2, TOK), jnp.int32),
            pltpu.VMEM((2, TOK), F32),
            pltpu.VMEM((HEADS, HD), F32),
            pltpu.VMEM((TOK * HEADS, HD), F32),
            pltpu.VMEM((TOK * HEADS, HD), F32),
            pltpu.VMEM((HEADS, TOK), F32),
            pltpu.VMEM((HEADS, SLAB, HD), BF),
            pltpu.VMEM((HEADS, SLAB, HD), BF),
            pltpu.VMEM((HEADS, HD, TOK), BF),
            pltpu.VMEM((HEADS, HD, TOK), BF),
            pltpu.VMEM((HEADS, TOK, HD), BF),
            pltpu.VMEM((MEM, HD + META, HD), BF),
            pltpu.VMEM((MEM, HD + META, HD), BF),
            pltpu.VMEM((8, HD, HD), BF),
            pltpu.VMEM((8, HD, HD), BF),
            pltpu.VMEM((2 * MEM, HD), F32),
            pltpu.VMEM((TILES * MEM, HD), F32),
            pltpu.VMEM((TILES * MEM, PAIR), F32),
            pltpu.VMEM((TILES * MEM, HD), F32),
            pltpu.VMEM((TILES, MEM, HD, HD), F32),
            pltpu.VMEM((TILES, MEM, HD, HD), BF),
            pltpu.VMEM((TILES, 2, HD, PAIR), F32),
            pltpu.VMEM((TILES, 2, PAIR, PAIR), F32),
            pltpu.VMEM((TILES, 8, PAIR), F32),
            *sems,
            pltpu.SemaphoreType.DMA((7,)),
        ],
        compiler_params=pltpu.CompilerParams(
            collective_id=0, has_side_effects=True, vmem_limit_bytes=60 * 1024 * 1024
        ),
        cost_estimate=pl.CostEstimate(
            flops=8 * 10**9, bytes_accessed=6 * 2**20, transcendentals=10**6
        ),
    )(
        queries[0],
        keys[0],
        values[0],
        log_decay[0].T,
        routes[0].T,
        route_weight[0].T,
        gain.reshape(HEADS, HD),
    )
    return jnp.swapaxes(out, 0, 1)[None]


def solution(mesh):
    finer = Mesh(mesh.devices.reshape(4, 2, 8, 4), ("mem_0", "mem_1", "ctx_0", "ctx_1"))
    ctx = ("ctx_0", "ctx_1")
    mem = ("mem_0", "mem_1")
    return jax.shard_map(
        shards,
        mesh=finer,
        in_specs=(
            P(ctx, mem, None, None),
            P(ctx, mem, None, None),
            P(ctx, mem, None, None),
            P(ctx, mem, None),
            P(ctx, mem, None),
            P(ctx, mem, None),
            P(),
        ),
        out_specs=P(ctx, mem, None, None),
        check_vma=False,
    )
```

```python
import jax
import jax.numpy as jnp
from jax import lax
from jax.experimental import pallas as pl
from jax.experimental.pallas import tpu as pltpu
from jax.sharding import Mesh
from jax.sharding import PartitionSpec as P

HEADS = 32
HD = 128
TOK = 128
MEM = 8
META = 16
PAIR = 2 * TOK
TILES = HEADS // 2
EARLY = 6
AHEAD = 2
ENOUGH = 12
SLAB = TOK + META + HD
BF = jnp.bfloat16
F32 = jnp.float32
SCALE = HD**-0.5
MESH = pl.DeviceIdType.MESH


def dot(a, b):
    return jnp.dot(a, b, preferred_element_type=F32)


ORDER = (
    ((0, 0), (1, 3), (3, 1), (2, 2), (1, 1), (3, 3), (1, 2), (3, 2))
    + ((2, 1), (2, 3), (0, 1), (1, 0), (0, 3), (3, 0), (0, 2), (2, 0))
)


def coded(values):
    whole = sum(v << (2 * i) for i, v in enumerate(values))
    return whole - (1 << 32) if whole >= 1 << 31 else whole


STEP_X, STEP_Y = coded([a for a, _ in ORDER]), coded([b for _, b in ORDER])


def offset(chip):
    if isinstance(chip, int):
        return ORDER[chip]
    turn = 2 * chip
    return tuple(jnp.bitwise_and(jnp.right_shift(jnp.int32(w), turn), 3) for w in (STEP_X, STEP_Y))


class Place:
    def __init__(self):
        self.x, self.y = lax.axis_index("ctx_1"), lax.axis_index("mem_0")
        self.c, self.z = lax.axis_index("mem_1"), lax.axis_index("ctx_0")
        self.me = (self.x * 4 + self.y) * 2 + self.c

    def target(self, chip, core):
        dx, dy = offset(chip)
        x, y, c = lax.rem(self.x + dx, 4), lax.rem(self.y + dy, 4), lax.rem(self.c + core, 2)
        return x * 4 + y, (x * 4 + y) * 2 + c, {"ctx_1": x, "mem_0": y, "mem_1": c}

    def source(self, chip, core):
        dx, dy = offset(chip)
        x, y, c = lax.rem(self.x + 4 - dx, 4), lax.rem(self.y + 4 - dy, 4), lax.rem(self.c + core, 2)
        return x * 4 + y, (x * 4 + y) * 2 + c

    def along(self, off):
        to = lax.rem(self.z + off, 8)
        return to, {"ctx_0": to}

    def back(self, off):
        return lax.rem(self.z + 8 - off, 8)


def remote(src, dst, sems, slot, device):
    return pltpu.make_async_remote_copy(
        src_ref=src,
        dst_ref=dst,
        send_sem=sems[0].at[slot],
        recv_sem=sems[1].at[slot],
        device_id=device,
        device_id_type=MESH,
    )


def loop(lo, hi, body):
    def step(i, _):
        body(i)
        return 0

    lax.fori_loop(lo, hi, step, 0)


def tile_meta(got, c):
    first = got[2 * c, TOK : TOK + META, :].astype(F32)
    second = got[2 * c + 1, TOK : TOK + META, :].astype(F32)
    return jnp.concatenate([first, second], axis=1)


def tile_masks(meta):
    ids = lax.broadcasted_iota(jnp.int32, (MEM, PAIR), 0).astype(F32)
    return jnp.where(meta[1:2, :] == ids, 1.0, 0.0), jnp.where(meta[2:3, :] == ids, 1.0, 0.0)


def pair_keys(got, c):
    return jnp.concatenate([got[2 * c, 0:TOK, :], got[2 * c + 1, 0:TOK, :]], axis=0)


def pair_values(got, c):
    return jnp.concatenate([got[2 * c, TOK + META :, :], got[2 * c + 1, TOK + META :, :]], axis=1)


def split_rows(rows):
    high = rows.astype(BF).astype(F32)
    return high, rows - high


def side_by_side(states):
    return jnp.concatenate([states[m] for m in range(MEM)], axis=1)


def chosen_queries(qt, oh):
    grouped = qt.reshape(HD // 16, 16, PAIR)
    parts = []
    for m in range(MEM):
        row = jnp.broadcast_to(oh[m : m + 1, :], (16, PAIR)).astype(BF)
        parts.append((grouped * row[None]).reshape(HD, PAIR))
    return jnp.concatenate(parts, axis=0)


def layer_kernel(
    q_ref,
    k_ref,
    v_ref,
    rate_ref,
    route_ref,
    weight_ref,
    gain_ref,
    out_ref,
    q_here,
    k_here,
    v_here,
    rate_here,
    route_here,
    weight_here,
    gain_here,
    flat_a,
    flat_b,
    rates,
    slabs,
    got,
    q_out,
    q_got,
    o_out,
    z_out,
    z_got,
    e_out,
    e_got,
    left,
    totals,
    sums,
    bases,
    incs,
    locals_,
    parts,
    decays,
    reaches,
    kv_s,
    kv_r,
    q_s,
    q_r,
    o_s,
    o_r,
    z_s,
    z_r,
    e_s,
    e_r,
    in_s,
):
    at = Place()
    me = at.me
    kv_sem, q_sem, o_sem, z_sem, e_sem = (kv_s, kv_r), (q_s, q_r), (o_s, o_r), (z_s, z_r), (e_s, e_r)

    fetches = [
        pltpu.make_async_copy(there, here, in_s.at[i])
        for i, (there, here) in enumerate(
            (
                (k_ref, k_here),
                (v_ref, v_here),
                (rate_ref, rate_here),
                (route_ref, route_here),
                (weight_ref, weight_here),
                (gain_ref, gain_here),
                (q_ref, q_here),
            )
        )
    ]
    for fetch in fetches:
        fetch.start()
    barrier = pltpu.get_barrier_semaphore()

    def greet(device):
        pl.semaphore_signal(barrier, inc=1, device_id=device, device_id_type=MESH)

    greet(at.target(0, 1)[2])
    loop(1, TILES, lambda t: [greet(at.target(t, core)[2]) for core in (0, 1)])
    loop(1, 8, lambda off: greet(at.along(off)[1]))

    def widen(flat, here):
        def some(i):
            rows = here[pl.ds(i * 16, 16), :, :].astype(F32)
            flat[pl.ds(i * 16 * HEADS, 16 * HEADS), :] = rows.reshape(16 * HEADS, HD)

        loop(0, TOK // 16, some)

    fetches[0].wait()
    widen(flat_a, k_here)
    fetches[1].wait()
    widen(flat_b, v_here)
    for fetch in fetches[2:]:
        fetch.wait()
    rates[...] = rate_here[...].astype(F32)
    row = lax.broadcasted_iota(jnp.int32, (META, TOK), 0)
    named = route_here[...].astype(F32)
    high, low = split_rows(weight_here[...])
    common = jnp.zeros((META, TOK), F32)
    lines = (named[0:1], named[1:2], high[0:1], low[0:1], high[1:2], low[1:2])
    for i, line in enumerate(lines):
        common = jnp.where(row == i + 1, line, common)

    def by_head(flat, d):
        return flat[pl.ds(d, TOK, stride=HEADS), :]

    def pack_kv(d, dest, slot):
        dest[slot, 0:TOK, :] = by_head(flat_a, d).astype(BF)
        dest[slot, TOK : TOK + META, :] = jnp.where(row == 0, rates[pl.ds(d, 1), :], common).astype(BF)
        dest[slot, TOK + META :, :] = by_head(flat_b, d).T.astype(BF)

    def kv_copy(chip, core):
        _, d, device = at.target(chip, core)
        return remote(slabs.at[d], got.at[me], kv_sem, 2 * chip + core, device)

    def pack_pair(t):
        for core in (0, 1):
            d = at.target(t, core)[1]
            pack_kv(d, slabs, d)

    def others(t, act):
        @pl.when(t > 0)
        def _():
            act(t, 0)

        act(t, 1)

    def start_pair(copy, t):
        others(t, lambda chip, core: copy(chip, core).start())

    def last_is_home(i):
        return lax.rem(i + 1, TILES)

    loop(0, EARLY, lambda i: pack_pair(i + 1))
    pl.semaphore_wait(barrier, 38)
    loop(0, EARLY, lambda i: start_pair(kv_copy, i + 1))

    def pack_and_start(i):
        pack_pair(last_is_home(i))
        start_pair(kv_copy, last_is_home(i))

    loop(EARLY, TILES, pack_and_start)
    got[me] = slabs[me]

    widen(flat_a, q_here)

    def q_copy(chip, core):
        _, d, device = at.target(chip, core)
        return remote(q_out.at[d], q_got.at[me], q_sem, 2 * chip + core, device)

    def pack_q(d, dest):
        dest[d] = by_head(flat_a, d).T.astype(BF)

    loop(0, TILES, lambda t: [pack_q(at.target(t, core)[1], q_out) for core in (0, 1)])
    q_got[me] = q_out[me]

    first = lax.broadcasted_iota(jnp.int32, (PAIR, PAIR), 0)
    second = lax.broadcasted_iota(jnp.int32, (PAIR, PAIR), 1)
    causal = first <= second

    def gather_tile(c):
        meta = tile_meta(got, c)
        oh0, oh1 = tile_masks(meta)
        mask = oh0 + oh1
        upper = jnp.where(causal, 1.0, 0.0).astype(BF)
        run = dot((mask * meta[0:1, :]).astype(BF), upper)
        sums[pl.ds(c * MEM, MEM), :] = run
        total = run[:, PAIR - 1 : PAIR]
        totals[pl.ds(c * MEM, MEM), :] = jnp.broadcast_to(total, (MEM, HD))
        kept = mask * jnp.exp(total - run)
        wide = pair_values(got, c).astype(F32)
        scaled = jnp.concatenate(
            [(wide * kept[m : m + 1, :]).astype(BF) for m in range(MEM)], axis=0
        )
        incs[c] = dot(scaled, pair_keys(got, c)).reshape(MEM, HD, HD)
        middle = 0.5 * total
        up = jnp.exp(run - middle) * SCALE
        reach = jnp.exp(run) * SCALE
        down_h, down_l = split_rows(mask * jnp.exp(middle - run))
        below = jnp.concatenate([down_h, down_l, down_h, down_l], axis=0).astype(BF)
        for j, oh in enumerate((oh0, oh1)):
            up_h, up_l = split_rows(oh * up)
            above = jnp.concatenate([up_h, up_h, up_l, up_l], axis=0).astype(BF)
            decay = lax.dot_general(
                below, above, (((0,), (0,)), ((), ())), preferred_element_type=F32
            )
            decays[c, j] = jnp.where(causal, decay, 0.0)
            reaches[c, j : j + 1, :] = jnp.sum(oh * reach, axis=0, keepdims=True)

    def arrived(t):
        others(t, lambda chip, core: kv_copy(chip, core).wait_recv())

        @pl.when(t == ENOUGH)
        def _():
            loop(0, TILES, lambda chip: start_pair(q_copy, chip))

        gather_tile(at.source(t, 0)[0])

    loop(0, TILES, arrived)

    whole = jnp.zeros((MEM, HD), F32)
    for c in range(TILES):
        lines = slice(c * MEM, (c + 1) * MEM)
        bases[lines, :] = whole
        total = totals[lines, :]
        totals[lines, :] = jnp.exp(total)
        whole = whole + total
    left_h, left_l = split_rows(jnp.exp(whole))
    left[0:MEM, :] = left_h
    left[MEM:, :] = left_l

    halves = (pl.ds(0, META + HD // 2), pl.ds(META + HD // 2, HD // 2))
    e_halves = (pl.ds(0, HD // 2), pl.ds(HD // 2, HD // 2))

    def z_copy(off, half):
        to, device = at.along(off)
        rows = halves[half]
        return remote(z_out.at[to, rows], z_got.at[at.z, rows], z_sem, 2 * off + half, device)

    def memory_states(m):
        def four(i, run):
            for k in range(4):
                c = 4 * i + k
                locals_[c, m] = run.astype(BF)
                run = run * totals[pl.ds(c * MEM + m, 1), :] + incs[c, m]
            return run

        run = lax.fori_loop(0, TILES // 4, four, jnp.zeros((HD, HD), F32))
        z_out[m, META:, :] = run.astype(BF)
        lines = left[pl.ds(m, 1), :], left[pl.ds(MEM + m, 1), :]
        z_out[m, 0:META, :] = jnp.where(row == 0, *lines).astype(BF)

    def send_states(off):
        memory_states(at.along(off)[0])
        z_copy(off, 0).start()

    loop(1, 8, send_states)
    loop(1, 8, lambda off: z_copy(off, 1).start())
    memory_states(at.z)
    z_got[at.z] = z_out[at.z]

    def inside_tile(c):
        meta = tile_meta(got, c)
        oh0, oh1 = tile_masks(meta)
        vt = pair_values(got, c)
        qt = jnp.concatenate([q_got[2 * c], q_got[2 * c + 1]], axis=1)
        scores = dot(pair_keys(got, c), qt)
        before = side_by_side(locals_.at[c])
        for j, oh in enumerate((oh0, oh1)):
            weights = (scores * decays[c, j]).astype(BF)
            across = dot(before, chosen_queries(qt, oh))
            parts[c, j] = dot(vt, weights) + across * reaches[c, j : j + 1, :]

    def e_copy(off, half):
        to, device = at.along(off)
        rows = e_halves[half]
        return remote(e_out.at[to, rows], e_got.at[at.z, rows], e_sem, 2 * off + half, device)

    def compose(half):
        loop(1, 8, lambda off: z_copy(off, half).wait_recv())
        entering = jnp.zeros((HD // 2, HD), F32)
        low = half * (HD // 2)
        rows = slice(low, low + HD // 2)
        given = slice(META + low, META + low + HD // 2)
        for z in range(8):
            e_out[z, rows, :] = entering.astype(BF)
            kept = z_got[z, 0:META, :].astype(F32)
            entering = entering * (kept[0:1, :] + kept[1:2, :]) + z_got[z, given, :].astype(F32)
        loop(1, 8, lambda off: e_copy(off, half).start())

    def compose_both():
        compose(0)
        compose(1)
        e_got[at.z] = e_out[at.z]

    def inside(i):
        pl.when(i == AHEAD)(compose_both)
        for t in (2 * i, 2 * i + 1):
            others(t, lambda chip, core: q_copy(chip, core).wait_recv())
        for t in (2 * i, 2 * i + 1):
            inside_tile(at.source(t, 0)[0])

    loop(0, TILES // 2, inside)
    for copy in (kv_copy, q_copy):
        sent = lambda chip, core, copy=copy: copy(chip, core).wait_send()
        loop(0, TILES, lambda t, sent=sent: others(t, sent))
    loop(1, 8, lambda off: [z_copy(off, half).wait_send() for half in (0, 1)])

    loop(1, 8, lambda off: [e_copy(off, half).wait_recv() for half in (0, 1)])
    gain = gain_here[pl.ds(me, 1), :]

    def finish_tile(c):
        meta = tile_meta(got, c)
        qt = jnp.concatenate([q_got[2 * c], q_got[2 * c + 1]], axis=1)
        base = bases[pl.ds(c * MEM, MEM), :][:, 0:1]
        reach = jnp.exp(sums[pl.ds(c * MEM, MEM), :] + base) * SCALE
        mixed = jnp.zeros((HD, PAIR), F32)
        for j, oh in enumerate(tile_masks(meta)):
            across = dot(side_by_side(e_got), chosen_queries(qt, oh))
            full = parts[c, j] + across * jnp.sum(oh * reach, axis=0, keepdims=True)
            square = jnp.mean(full * full, axis=0, keepdims=True)
            weight = meta[3 + 2 * j : 4 + 2 * j, :] + meta[4 + 2 * j : 5 + 2 * j, :]
            mixed = mixed + full * (lax.rsqrt(square + 1e-06) * weight)
        return (mixed.T * gain).astype(BF)

    def o_copy(chip, core):
        _, d, device = at.target(chip, core)
        return remote(o_out.at[d], out_ref.at[me], o_sem, 0, device)

    def finish(i):
        t = last_is_home(i)
        c = at.target(t, 0)[0]
        done = finish_tile(c)
        o_out[2 * c] = done[0:TOK]
        o_out[2 * c + 1] = done[TOK:]
        start_pair(o_copy, t)

    loop(0, TILES, finish)
    own = pltpu.make_async_copy(o_out.at[me], out_ref.at[me], in_s.at[0])
    own.start()
    loop(1, 8, lambda off: [e_copy(off, half).wait_send() for half in (0, 1)])
    own.wait()
    every = pl.ds(0, HEADS - 1)
    whole_out = remote(o_out.at[every], out_ref.at[every], o_sem, 0, at.target(0, 1)[2])
    whole_out.wait_recv()
    whole_out.wait_send()


def shards(queries, keys, values, log_decay, routes, route_weight, gain):
    sems = [pltpu.SemaphoreType.DMA((HEADS,))] * 4 + [pltpu.SemaphoreType.DMA((1,))] * 2 + [pltpu.SemaphoreType.DMA((16,))] * 4
    out = pl.pallas_call(
        layer_kernel,
        out_shape=jax.ShapeDtypeStruct((HEADS, TOK, HD), BF),
        in_specs=[pl.BlockSpec(memory_space=pltpu.HBM)] * 7,
        out_specs=pl.BlockSpec(memory_space=pltpu.HBM),
        scratch_shapes=[
            pltpu.VMEM((TOK, HEADS, HD), BF),
            pltpu.VMEM((TOK, HEADS, HD), BF),
            pltpu.VMEM((TOK, HEADS, HD), BF),
            pltpu.VMEM((HEADS, TOK), BF),
            pltpu.VMEM((2, TOK), jnp.int32),
            pltpu.VMEM((2, TOK), F32),
            pltpu.VMEM((HEADS, HD), F32),
            pltpu.VMEM((TOK * HEADS, HD), F32),
            pltpu.VMEM((TOK * HEADS, HD), F32),
            pltpu.VMEM((HEADS, TOK), F32),
            pltpu.VMEM((HEADS, SLAB, HD), BF),
            pltpu.VMEM((HEADS, SLAB, HD), BF),
            pltpu.VMEM((HEADS, HD, TOK), BF),
            pltpu.VMEM((HEADS, HD, TOK), BF),
            pltpu.VMEM((HEADS, TOK, HD), BF),
            pltpu.VMEM((MEM, HD + META, HD), BF),
            pltpu.VMEM((MEM, HD + META, HD), BF),
            pltpu.VMEM((8, HD, HD), BF),
            pltpu.VMEM((8, HD, HD), BF),
            pltpu.VMEM((2 * MEM, HD), F32),
            pltpu.VMEM((TILES * MEM, HD), F32),
            pltpu.VMEM((TILES * MEM, PAIR), F32),
            pltpu.VMEM((TILES * MEM, HD), F32),
            pltpu.VMEM((TILES, MEM, HD, HD), F32),
            pltpu.VMEM((TILES, MEM, HD, HD), BF),
            pltpu.VMEM((TILES, 2, HD, PAIR), F32),
            pltpu.VMEM((TILES, 2, PAIR, PAIR), F32),
            pltpu.VMEM((TILES, 8, PAIR), F32),
            *sems,
            pltpu.SemaphoreType.DMA((7,)),
        ],
        compiler_params=pltpu.CompilerParams(
            collective_id=0, has_side_effects=True, vmem_limit_bytes=60 * 1024 * 1024
        ),
        cost_estimate=pl.CostEstimate(
            flops=8 * 10**9, bytes_accessed=6 * 2**20, transcendentals=10**6
        ),
    )(
        queries[0],
        keys[0],
        values[0],
        log_decay[0].T,
        routes[0].T,
        route_weight[0].T,
        gain.reshape(HEADS, HD),
    )
    return jnp.swapaxes(out, 0, 1)[None]


def solution(mesh):
    finer = Mesh(mesh.devices.reshape(4, 2, 8, 4), ("mem_0", "mem_1", "ctx_0", "ctx_1"))
    ctx = ("ctx_0", "ctx_1")
    mem = ("mem_0", "mem_1")
    return jax.shard_map(
        shards,
        mesh=finer,
        in_specs=(
            P(ctx, mem, None, None),
            P(ctx, mem, None, None),
            P(ctx, mem, None, None),
            P(ctx, mem, None),
            P(ctx, mem, None),
            P(ctx, mem, None),
            P(),
        ),
        out_specs=P(ctx, mem, None, None),
        check_vma=False,
    )
```
